32 devices in a mesh: parts: 2 (over x), dp: 16 (over z, y, core).
Axes of the slice: x: 2, y: 2, z: 4, core: 2. Of those that a mesh axis runs over, the one named last changes fastest.
Arguments:
- cache_keys: bfloat16 [128, 256, 512], P(('parts', 'dp')), parts along dimension 0, may hold values from -6 to 6
- cache_values: bfloat16 [128, 256, 512], P(('parts', 'dp')), parts along dimension 0, may hold values from -6 to 6
- lengths: int32 [128], P(('parts', 'dp')), parts along dimension 0, may hold values from 1 to 255
- unfinished: int32 [128], P(('parts', 'dp')), parts along dimension 0, may hold values from 0 to 1
- send_slot: int32 [32], P('parts'), parts along dimension 0, may hold values from 0 to 3, as said below
- send_to: int32 [32], P('parts'), parts along dimension 0, may hold values from 0 to 15, as said below
- receive_from: int32 [32], P('parts'), parts along dimension 0, may hold values from 0 to 15, as said below
- land_slot: int32 [32], P('parts'), parts along dimension 0, may hold values from 0 to 3, as said below
- land_length: int32 [32], P('parts'), parts along dimension 0, may hold values from 1 to 255, as said below
- queries: bfloat16 [128, 4096], P(('parts', 'dp')), parts along dimension 0
- new_keys: bfloat16 [128, 512], P(('parts', 'dp')), parts along dimension 0
- new_values: bfloat16 [128, 512], P(('parts', 'dp')), parts along dimension 0, may hold values from -6 to 6
- norm_gain: float32 [4096], replicated, may hold values from 0.1 to 1.9
- gate_weight: bfloat16 [4096, 4096], P(None, 'dp'), may hold values from -0.09375 to 0.09375
- up_weight: bfloat16 [4096, 4096], P(None, 'dp'), may hold values from -0.09375 to 0.09375
- down_weight: bfloat16 [4096, 4096], P('dp'), may hold values from -0.125 to 0.125
Outputs:
- decoded: bfloat16 [128, 4096], P(('parts', 'dp')), parts along dimension 0
- keys_after: bfloat16 [128, 256, 512], P(('parts', 'dp')), parts along dimension 0
- values_after: bfloat16 [128, 256, 512], P(('parts', 'dp')), parts along dimension 0
The draws below stay inside these ranges and needn't reach their ends.
There are 2 independent parts, one for each index of `parts`. The reference program is written for one: setup_inputs(seed, part) draws one part's arguments, and reference() takes and returns one part's arrays. A program takes and returns all parts, laid end to end along the dimension named above; an argument that names none is the same for every part. Nothing has to cross between parts.
Inputs may be any that keep to these rules, and one draw needn't show every extreme that they name: No replica both gives and receives; on a giving replica r, send_to[r] is a receiving replica. `receive_from`: on a receiving replica r, the giving replica s with send_to[s] = r. `send_slot`: on a giving replica, the slot of an unfinished sequence. `land_slot`: on a receiving replica, a slot whose sequence is finished. `land_length`: equals lengths at row receive_from[r] * 4 + send_slot[receive_from[r]].
All inputs are finite; a program needn't handle non-finite values.
Results may differ from the reference program's by a relative error of at most 0.0078.
Values may be sent and summed in bfloat16 or wider, within the bound.
No kernel may reach another device: no remote copies, remote signals or barrier semaphores. Data moves between devices by JAX's collectives and lax.ppermute only.
A program may use at most 192 MiB of HBM per device.

```python
import jax
import jax.numpy as jnp
from jax import lax

HQ = 32
KVH = 4
HD = 128
SLOTS = 4
CAP = 256
D = 4096
KVW = 512
FF = 4096
ROWS = 64
N_DP = 16


def plan_lists(key):
    replica_ids = jnp.arange(N_DP, dtype=jnp.int32)
    order = jax.random.permutation(jax.random.fold_in(key, 101), N_DP).astype(jnp.int32)
    ranking = jnp.zeros((N_DP,), jnp.int32).at[order].set(replica_ids)
    movers = N_DP // 4
    sender = ranking < movers
    receiver = (ranking >= movers) & (ranking < 2 * movers)
    send_to = jnp.where(sender, order[jnp.clip(ranking + movers, 0, N_DP - 1)], replica_ids)
    receive_from = jnp.where(receiver, order[jnp.clip(ranking - movers, 0, N_DP - 1)], replica_ids)
    send_slot = jax.random.randint(jax.random.fold_in(key, 102), (N_DP,), 0, SLOTS).astype(jnp.int32)
    land_slot = jax.random.randint(jax.random.fold_in(key, 103), (N_DP,), 0, SLOTS).astype(jnp.int32)
    flags = (jax.random.randint(jax.random.fold_in(key, 104), (N_DP, SLOTS), 0, 4) > 0).astype(jnp.int32)
    flags = jnp.where(sender[:, None], 1, flags)
    flags = jnp.where(receiver[:, None], 0, flags)
    short_lengths = jax.random.randint(jax.random.fold_in(key, 105), (N_DP, SLOTS), 1, CAP)
    long_lengths = jax.random.randint(jax.random.fold_in(key, 106), (N_DP, SLOTS), CAP // 2, CAP)
    length_table = jnp.where(sender[:, None], long_lengths, short_lengths).astype(jnp.int32)
    leader = order[0]
    length_table = length_table.at[leader, send_slot[leader]].set(CAP - 1)
    length_flat = length_table.reshape(-1)
    land_length = length_flat[receive_from * SLOTS + send_slot[receive_from]]
    return (length_flat, flags.reshape(-1), send_slot, send_to, receive_from, land_slot, land_length)


def key_rows(key):
    return jax.random.normal(jax.random.fold_in(key, 201), (N_DP * SLOTS, KVH * HD), jnp.float32)


def draw_lengths(key, part):
    return plan_lists(key)[0]


def draw_unfinished(key, part):
    return plan_lists(key)[1]


def draw_send_slot(key, part):
    return plan_lists(key)[2]


def draw_send_to(key, part):
    return plan_lists(key)[3]


def draw_receive_from(key, part):
    return plan_lists(key)[4]


def draw_land_slot(key, part):
    return plan_lists(key)[5]


def draw_land_length(key, part):
    return plan_lists(key)[6]


def draw_new_keys(key, part):
    return key_rows(key).astype(jnp.bfloat16)


def draw_queries(key, part):
    key = jax.random.fold_in(key, 12)
    base = jax.random.normal(key, (N_DP * SLOTS, HQ * HD), jnp.float32)
    return base.astype(jnp.bfloat16)


def with_spikes(array, stream_key, source, target, blocks, factor):
    def block_of(axis_at):
        return (jnp.arange(array.shape[axis_at]) // (array.shape[axis_at] // blocks)).reshape((-1,) + (1,) * (array.ndim - 1 - axis_at))

    one_side = jax.random.permutation(stream_key, blocks)[block_of(target)]
    far = (block_of(target) + blocks // 2) % blocks
    return jnp.where((block_of(source) == one_side) | (block_of(source) == far), factor * array, array)


def block_scale(own_key, dims, shards, smallest, largest):
    factor_of, own = 1.0, jax.random.fold_in(own_key, 6)
    for position, parts in shards:
        draws = jnp.exp(jax.random.uniform(jax.random.fold_in(own, position), (parts,), jnp.float32, smallest / len(shards), largest / len(shards)))
        factor_of = factor_of * jnp.repeat(draws, dims[position] // parts).reshape([-1 if axis == position else 1 for axis in range(len(dims))])
    return factor_of


def gaussian(key, dims, width, bound, cuts=(), held_as=jnp.bfloat16):
    level = block_scale(key, dims, cuts, -0.22, 0.18) if cuts else 1.0
    drawn = jax.random.normal(key, dims, jnp.float32) * width * level
    return jnp.minimum(jnp.maximum(drawn, -bound), bound).astype(held_as)


def heavy_noise(stream_key, extent, scale, most, shards, heavy, kind=jnp.bfloat16):
    values = scale * jax.random.normal(stream_key, extent, jnp.float32)
    if shards:
        values = values * block_scale(stream_key, extent, shards, -0.22, 0.18)
    return jnp.clip(with_spikes(values, jax.random.fold_in(stream_key, 3), *heavy), -most, most).astype(kind)


def setup_inputs(seed: int = 0, part: int = 0) -> dict:
    arg_keys = jax.random.split(jax.random.key(seed), 17)
    own_keys = jax.random.split(jax.random.fold_in(arg_keys[16], part), 17)
    cache_keys = gaussian(own_keys[0], (ROWS, CAP, KVW), 1.0, 6.0, ((0, 16),))
    cache_values = gaussian(own_keys[1], (ROWS, CAP, KVW), 1.0, 6.0, ((0, 16),))
    lengths = draw_lengths(jax.random.fold_in(jax.random.fold_in(arg_keys[16], part), 71), part)
    unfinished = draw_unfinished(jax.random.fold_in(jax.random.fold_in(arg_keys[16], part), 71), part)
    send_slot = draw_send_slot(jax.random.fold_in(jax.random.fold_in(arg_keys[16], part), 71), part)
    send_to = draw_send_to(jax.random.fold_in(jax.random.fold_in(arg_keys[16], part), 71), part)
    receive_from = draw_receive_from(jax.random.fold_in(jax.random.fold_in(arg_keys[16], part), 71), part)
    land_slot = draw_land_slot(jax.random.fold_in(jax.random.fold_in(arg_keys[16], part), 71), part)
    land_length = draw_land_length(jax.random.fold_in(jax.random.fold_in(arg_keys[16], part), 71), part)
    queries = draw_queries(jax.random.fold_in(jax.random.fold_in(arg_keys[16], part), 71), part)
    new_keys = draw_new_keys(jax.random.fold_in(jax.random.fold_in(arg_keys[16], part), 71), part)
    new_values = gaussian(own_keys[11], (ROWS, KVW), 1.0, 6.0, ((0, 16),))
    norm_gain = jnp.clip(1.0 + 0.18 * jax.random.normal(arg_keys[12], (D,), jnp.float32), 0.1, 1.9)
    gate_weight = gaussian(arg_keys[13], (D, FF), D ** -0.5, 0.09375, ((1, 16),))
    up_weight = gaussian(arg_keys[14], (D, FF), D ** -0.5, 0.09375, ((1, 16),))
    down_weight = heavy_noise(arg_keys[15], (FF, D), FF ** -0.5, 0.125, ((0, 16),), (0, 1, 16, 2.0))
    return {"cache_keys": cache_keys, "cache_values": cache_values, "lengths": lengths, "unfinished": unfinished, "send_slot": send_slot, "send_to": send_to, "receive_from": receive_from, "land_slot": land_slot, "land_length": land_length, "queries": queries, "new_keys": new_keys, "new_values": new_values, "norm_gain": norm_gain, "gate_weight": gate_weight, "up_weight": up_weight, "down_weight": down_weight}


def reference(cache_keys, cache_values, lengths, unfinished, send_slot, send_to, receive_from, land_slot, land_length, queries, new_keys, new_values, norm_gain, gate_weight, up_weight, down_weight):
    row_total = N_DP * SLOTS
    replica_ids = jnp.arange(N_DP, dtype=jnp.int32)
    arriving = receive_from != replica_ids
    giving = send_to != replica_ids
    source_row = (receive_from * SLOTS + send_slot[receive_from]).astype(jnp.int32)
    landing = (replica_ids * SLOTS + land_slot).astype(jnp.int32)
    vacated = (replica_ids * SLOTS + send_slot).astype(jnp.int32)
    row_map = jnp.arange(row_total, dtype=jnp.int32).at[landing].set(jnp.where(arriving, source_row, landing))
    moved_keys = cache_keys[row_map]
    moved_values = cache_values[row_map]
    length_now = lengths.at[landing].set(jnp.where(arriving, land_length, lengths[landing]))
    alive = unfinished.at[landing].set(jnp.where(arriving, 1, unfinished[landing]))
    alive = alive.at[vacated].set(jnp.where(giving, 0, alive[vacated]))
    group = HQ // KVH
    scale = 1.0 / HD ** 0.5

    def one_block(block):
        key_block, value_block, query_block, key_new, value_new, length_block, alive_block = block
        positions = jnp.arange(CAP, dtype=jnp.int32)
        append = (positions[None, :] == length_block[:, None]) & (alive_block[:, None] > 0)
        key_block = jnp.where(append[:, :, None], key_new[:, None, :], key_block)
        value_block = jnp.where(append[:, :, None], value_new[:, None, :], value_block)
        query_heads = query_block.astype(jnp.float32).reshape(SLOTS, KVH, group, HD)
        key_heads = key_block.astype(jnp.float32).reshape(SLOTS, CAP, KVH, HD)
        value_heads = value_block.astype(jnp.float32).reshape(SLOTS, CAP, KVH, HD)
        scores = jnp.einsum('skgd,sckd->skgc', query_heads, key_heads) * scale
        visible = (positions[None, :] <= length_block[:, None])[:, None, None, :]
        scores = jnp.where(visible, scores, jnp.float32(-1e+30))
        top = lax.optimization_barrier(jnp.max(scores, axis=-1, keepdims=True))
        expo = jnp.exp(scores - top)
        probs = (expo / lax.optimization_barrier(jnp.sum(expo, axis=-1, keepdims=True))).astype(jnp.bfloat16)
        probs = lax.optimization_barrier(probs).astype(jnp.float32)
        attended = jnp.einsum('skgc,sckd->skgd', probs, value_heads).reshape(SLOTS, HQ * HD)
        mean_square = lax.optimization_barrier(jnp.mean(attended * attended, axis=-1, keepdims=True))
        normed = attended * lax.rsqrt(mean_square + 1e-06) * norm_gain.astype(jnp.float32)[None, :]
        normed = jnp.where(alive_block[:, None] > 0, normed, 0.0).astype(jnp.bfloat16)
        return (key_block, value_block, normed)
    blocks = (moved_keys.reshape(N_DP, SLOTS, CAP, KVH * HD), moved_values.reshape(N_DP, SLOTS, CAP, KVH * HD), queries.reshape(N_DP, SLOTS, HQ * HD), new_keys.reshape(N_DP, SLOTS, KVH * HD), new_values.reshape(N_DP, SLOTS, KVH * HD), length_now.reshape(N_DP, SLOTS), alive.reshape(N_DP, SLOTS))
    keys_after, values_after, normed = lax.map(one_block, blocks)
    normed = normed.reshape(row_total, HQ * HD)
    gate = jnp.dot(normed, gate_weight, preferred_element_type=jnp.float32)
    up_part = jnp.dot(normed, up_weight, preferred_element_type=jnp.float32)
    hidden = (jax.nn.silu(gate) * up_part).astype(jnp.bfloat16)
    decoded = jnp.dot(hidden, down_weight, preferred_element_type=jnp.float32).astype(jnp.bfloat16)
    return (decoded, keys_after.reshape(row_total, CAP, KVH * HD), values_after.reshape(row_total, CAP, KVH * HD))
```

```python
import math

import jax
import jax.numpy as jnp
from jax import lax
from jax.sharding import PartitionSpec as P

HQ = 32
KVH = 4
HD = 128


def exchange(blocks, axis):
    return lax.all_to_all(blocks, axis, 0, 0, tiled=True)


def per_device(
    cache_keys,
    cache_values,
    lengths,
    unfinished,
    send_slot,
    send_to,
    receive_from,
    land_slot,
    land_length,
    queries,
    new_keys,
    new_values,
    norm_gain,
    gate_weight,
    up_weight,
    down_weight,
):
    group = ("chip", "core")
    me = lax.axis_index(group)
    chips, n = lax.axis_size("chip"), lax.axis_size(group)
    my_chip, my_core = lax.axis_index("chip"), lax.axis_index("core")
    slots, capacity, kv_width = cache_keys.shape
    width = queries.shape[1]
    slot_ids = jnp.arange(slots)
    target, source = send_to[me], receive_from[me]
    given_slot, taken_slot = send_slot[me], land_slot[me]
    giving, arriving = target != me, source != me
    landing = (slot_ids == taken_slot) & arriving
    vacated = (slot_ids == given_slot) & giving

    packet = jnp.concatenate(
        [
            lax.dynamic_index_in_dim(queries, taken_slot, 0, keepdims=False),
            lax.dynamic_index_in_dim(new_keys, taken_slot, 0, keepdims=False),
            lax.dynamic_index_in_dim(new_values, taken_slot, 0, keepdims=False),
        ]
    ).reshape(-1, 128)
    packets = exchange(jnp.broadcast_to(packet[None], (n,) + packet.shape), group)
    got = lax.dynamic_index_in_dim(packets, target, 0, keepdims=False).reshape(-1)

    rows = capacity // n
    leaving = jnp.concatenate(
        [
            lax.dynamic_index_in_dim(cache_keys, given_slot, 0, keepdims=False).reshape(n, rows, kv_width),
            lax.dynamic_index_in_dim(cache_values, given_slot, 0, keepdims=False).reshape(n, rows, kv_width),
        ],
        axis=1,
    )
    spread = exchange(leaving, group)

    row_queries = jnp.where(vacated[:, None], got[None, :width], queries)
    row_keys = jnp.where(vacated[:, None], got[None, width : width + kv_width], new_keys)
    row_values = jnp.where(vacated[:, None], got[None, width + kv_width :], new_values)
    row_alive = jnp.where(vacated, 1, jnp.where(landing, 0, unfinished)) > 0
    positions = jnp.arange(capacity)
    append = (positions[None, :] == lengths[:, None]) & row_alive[:, None]
    keys_here = jnp.where(append[:, :, None], row_keys[:, None, :], cache_keys)
    values_here = jnp.where(append[:, :, None], row_values[:, None, :], cache_values)
    query_heads = row_queries.reshape(slots, KVH, HQ // KVH, HD)
    key_heads = keys_here.reshape(slots, capacity, KVH, HD)
    value_heads = values_here.reshape(slots, capacity, KVH, HD)
    scores = jnp.einsum(
        "skgd,sckd->skgc", query_heads, key_heads, preferred_element_type=jnp.float32
    ) * (1.0 / math.sqrt(HD))
    visible = (positions[None, :] <= lengths[:, None])[:, None, None, :]
    scores = jnp.where(visible, scores, jnp.float32(-1e30))
    top = jnp.max(scores, axis=-1, keepdims=True)
    expo = jnp.exp(scores - top)
    probs = (expo / jnp.sum(expo, axis=-1, keepdims=True)).astype(jnp.bfloat16)
    attended = jnp.einsum(
        "skgc,sckd->skgd", probs, value_heads, preferred_element_type=jnp.float32
    ).reshape(slots, HQ * HD)
    mean_square = jnp.mean(attended * attended, axis=-1, keepdims=True)
    normed = attended * lax.rsqrt(mean_square + 1e-06) * norm_gain[None, :]
    normed = jnp.where(row_alive[:, None], normed, 0.0).astype(jnp.bfloat16)

    by_chip = exchange(jnp.broadcast_to(normed[None], (chips,) + normed.shape), "chip")
    other = lax.ppermute(by_chip, "core", [(0, 1), (1, 0)])

    chosen = jnp.take(spread, jnp.clip(receive_from, 0, n - 1), axis=0)
    arrived = exchange(chosen, group)
    arrived_keys = arrived[:, :rows].reshape(capacity, kv_width)
    arrived_values = arrived[:, rows:].reshape(capacity, kv_width)
    length_now = jnp.where(landing, land_length[me], lengths)
    alive = jnp.where(vacated, 0, jnp.where(landing, 1, unfinished)) > 0
    append_now = (positions[None, :] == length_now[:, None]) & alive[:, None]
    keys_after = jnp.where(landing[:, None, None], arrived_keys[None], cache_keys)
    values_after = jnp.where(landing[:, None, None], arrived_values[None], cache_values)
    keys_after = jnp.where(append_now[:, :, None], new_keys[:, None, :], keys_after)
    values_after = jnp.where(append_now[:, :, None], new_values[:, None, :], values_after)

    gathered = jnp.concatenate([by_chip, other], axis=0).reshape(n * slots, width)
    gate = jnp.dot(gathered, gate_weight, preferred_element_type=jnp.float32)
    up_part = jnp.dot(gathered, up_weight, preferred_element_type=jnp.float32)
    hidden = (jax.nn.silu(gate) * up_part).astype(jnp.bfloat16)
    everyone = jnp.arange(n)
    arrives = receive_from != everyone
    gives = send_to != everyone
    row_of = everyone[:, None] * slots + slot_ids[None, :]
    from_row = jnp.where(
        arrives[:, None] & (slot_ids[None, :] == land_slot[:, None]),
        (receive_from * slots + jnp.take(send_slot, jnp.clip(receive_from, 0, n - 1)))[:, None],
        row_of,
    )
    from_row = jnp.where(gives[:, None] & (slot_ids[None, :] == send_slot[:, None]), -1, from_row)
    order = jnp.concatenate([jnp.arange(chips) * 2 + 1 - my_core, jnp.arange(chips) * 2 + my_core])
    held = jnp.concatenate([jnp.arange(chips) * 2 + my_core, jnp.arange(chips) * 2 + 1 - my_core])
    wanted = jnp.take(from_row, order, axis=0).reshape(-1)
    held_row = (held[:, None] * slots + slot_ids[None, :]).reshape(-1)
    pick = (wanted[:, None] == held_row[None, :]).astype(jnp.bfloat16)
    placed_hidden = jnp.dot(pick, hidden, preferred_element_type=jnp.float32).astype(jnp.bfloat16)
    partial = jnp.dot(placed_hidden, down_weight, preferred_element_type=jnp.float32)
    half = chips * slots
    from_other = lax.ppermute(partial[:half].astype(jnp.bfloat16), "core", [(0, 1), (1, 0)])
    chip_sum = (partial[half:] + from_other.astype(jnp.float32)).astype(jnp.bfloat16)
    pieces = exchange(chip_sum.reshape(chips, slots, width), "chip")
    decoded = jnp.sum(pieces.astype(jnp.float32), axis=0).astype(jnp.bfloat16)
    return (decoded, keys_after, values_after)


def solution(mesh):
    parts, n = mesh.shape["parts"], mesh.shape["dp"]
    split = jax.sharding.Mesh(mesh.devices.reshape(parts, n // 2, 2), ("parts", "chip", "core"))
    every, own = ("parts", "chip", "core"), ("chip", "core")
    placed = (
        P(every, None, None),
        P(every, None, None),
        P(every),
        P(every),
        P("parts"),
        P("parts"),
        P("parts"),
        P("parts"),
        P("parts"),
        P(every, None),
        P(every, None),
        P(every, None),
        P(),
        P(None, own),
        P(None, own),
        P(own, None),
    )
    return jax.shard_map(
        per_device,
        mesh=split,
        in_specs=placed,
        out_specs=(P(every, None), P(every, None, None), P(every, None, None)),
        check_vma=False,
    )
```

```python
import functools
import math

import jax
import jax.numpy as jnp
from jax import lax
from jax.experimental import pallas as pl
from jax.experimental.pallas import tpu as pltpu
from jax.sharding import PartitionSpec as P

HQ = 32
KVH = 4
HD = 128
TILE = 16
GROUP = ("chip", "core")
SMEM, VMEM = pltpu.SMEM, pltpu.VMEM


def exchange(blocks, axis):
    return lax.all_to_all(blocks, axis, 0, 0, tiled=True)


def spec(space):
    return pl.BlockSpec(memory_space=space)


def cost(flops, moved):
    return pl.CostEstimate(flops=flops, bytes_accessed=moved, transcendentals=0)


def pack_kernel(send_slot, land_slot, q, nk, nv, ck, cv, packets, leaving, lines, sems):
    me = lax.axis_index(GROUP)
    n, slots = packets.shape[0], q.shape[1]
    given, taken = send_slot[me], land_slot[me]
    copies = [
        pltpu.make_async_copy(ck.at[given], leaving.at[:, pl.ds(0, TILE)], sems.at[0]),
        pltpu.make_async_copy(cv.at[given], leaving.at[:, pl.ds(TILE, TILE)], sems.at[1]),
    ]
    for copy in copies:
        copy.start()
    lines[...] = jnp.zeros_like(lines)
    at = 0
    for x in (q, nk, nv):
        heads = x.shape[0]
        mine = lax.broadcasted_iota(jnp.int32, (heads, slots, HD), 1) == taken
        lines[at : at + heads] = jnp.sum(jnp.where(mine, x[...].astype(jnp.float32), 0.0), axis=1)
        at += heads
    packet = lines[...].astype(jnp.bfloat16)
    for d in range(n):
        packets[d] = packet
    for copy in copies:
        copy.wait()


def attend_kernel(
    send_slot, send_to, lengths, unfinished, packets, q, nk, nv, gain, ck, cv, out, kbuf, vbuf, q32, att, sems
):
    me = lax.axis_index(GROUP)
    slots, capacity, _ = ck.shape
    loads = []
    for j in range(slots):
        loads.append(
            (
                pltpu.make_async_copy(ck.at[j], kbuf.at[j], sems.at[0, j]),
                pltpu.make_async_copy(cv.at[j], vbuf.at[j], sems.at[1, j]),
            )
        )
        for copy in loads[j]:
            copy.start()
    target, given = send_to[me], send_slot[me]
    packet = packets[target].astype(jnp.float32)
    q32[...] = q[...].astype(jnp.float32)
    nk32, nv32 = nk[...].astype(jnp.float32), nv[...].astype(jnp.float32)
    scale = 1.0 / math.sqrt(HD)
    per = HQ // KVH
    for j in range(slots):
        moved = (target != me) & (given == j)
        alive = jnp.where(moved, 1, unfinished[j]) > 0
        length = lengths[j]
        base = pl.multiple_of((length // TILE) * TILE, TILE)
        line = jnp.where(alive, length - base, -1)
        here = lax.broadcasted_iota(jnp.int32, (TILE, HD), 0) == line
        for copy in loads[j]:
            copy.wait()
        for k in range(KVH):
            columns = slice(k * HD, (k + 1) * HD)
            for buf, own, at in ((kbuf, nk32, HQ + k), (vbuf, nv32, HQ + KVH + k)):
                fresh = jnp.where(moved, packet[at : at + 1], own[k, j : j + 1])
                block = buf[j, pl.ds(base, TILE), columns].astype(jnp.float32)
                buf[j, pl.ds(base, TILE), columns] = jnp.where(here, fresh, block).astype(jnp.bfloat16)
        qj = jnp.where(moved, packet[:HQ], q32[:, j, :])
        scores = jnp.concatenate(
            [
                lax.dot_general(
                    qj[k * per : (k + 1) * per].astype(jnp.bfloat16),
                    kbuf[j, :, k * HD : (k + 1) * HD],
                    (((1,), (1,)), ((), ())),
                    preferred_element_type=jnp.float32,
                )
                for k in range(KVH)
            ],
            axis=0,
        )
        visible = lax.broadcasted_iota(jnp.int32, scores.shape, 1) <= length
        scores = jnp.where(visible, scores * scale, jnp.float32(-1e30))
        expo = jnp.exp(scores - jnp.max(scores, axis=1, keepdims=True))
        probs = expo / jnp.sum(expo, axis=1, keepdims=True)
        attended = jnp.concatenate(
            [
                jnp.dot(
                    probs[k * per : (k + 1) * per].astype(jnp.bfloat16),
                    vbuf[j, :, k * HD : (k + 1) * HD],
                    preferred_element_type=jnp.float32,
                )
                for k in range(KVH)
            ],
            axis=0,
        )
        mean = jnp.sum(attended * attended, keepdims=True) * (1.0 / (HQ * HD))
        normed = attended * lax.rsqrt(mean + 1e-06) * gain[...]
        att[:, j, :] = jnp.where(alive, normed, 0.0)
    for h in range(HQ):
        head = att[h].astype(jnp.bfloat16)
        for c in range(out.shape[0]):
            out[c, :, h * HD : (h + 1) * HD] = head


def select_kernel(send_slot, send_to, receive_from, land_slot, spread, _, chosen, pick, sem):
    n = chosen.shape[0]
    rows = pick.shape[0]
    half, slots = rows // 2, rows // n
    core = lax.axis_index("core")

    def copy(d):
        return pltpu.make_async_copy(spread.at[receive_from[d]], chosen.at[d], sem.at[d])

    for d in range(n):
        pl.when(receive_from[d] != d)(lambda d=d: copy(d).start())
    row = lax.broadcasted_iota(jnp.int32, (rows, HD), 0)
    wanted = jnp.where(row < half, row + half, row - half)
    for d in range(n):
        same = lax.rem(d, 2) == core
        there = jnp.where(same, half, 0) + (d // 2) * slots
        source = receive_from[d]
        held = jnp.where(lax.rem(source, 2) == core, 0, half) + (source // 2) * slots + send_slot[source]
        landing = jnp.where(source != d, there + land_slot[d], -1)
        vacated = jnp.where(send_to[d] != d, there + send_slot[d], -1)
        wanted = jnp.where(row == landing, held, wanted)
        wanted = jnp.where(row == vacated, -1, wanted)
    column = lax.broadcasted_iota(jnp.int32, (rows, rows), 1)
    pick[...] = (column == wanted[:, :1]).astype(jnp.float32).astype(jnp.bfloat16)
    for d in range(n):
        pl.when(receive_from[d] != d)(lambda d=d: copy(d).wait())


def merge_kernel(
    send_slot, send_to, receive_from, land_slot, land_length, lengths, unfinished, nk, nv, ck, cv, arrived, _,
    keys, values, lines, sems
):
    me = lax.axis_index(GROUP)
    slots = ck.shape[0]
    source, target = receive_from[me], send_to[me]
    plans = []
    for j in range(slots):
        landing = (source != me) & (land_slot[me] == j)
        vacated = (target != me) & (send_slot[me] == j)
        length = jnp.where(landing, land_length[me], lengths[j])
        alive = jnp.where(vacated, 0, jnp.where(landing, 1, unfinished[j])) > 0
        plans.append((landing, length // TILE, lax.rem(length, TILE), alive))

    def copies(j, landed):
        block = plans[j][1]
        made = []
        for i, (cache, out) in enumerate(((ck, keys), (cv, values))):
            whole = arrived.at[:, pl.ds(i * TILE, TILE)] if landed else cache.at[j]
            piece = arrived.at[block, pl.ds(i * TILE, TILE)] if landed else cache.at[j, block]
            made.append(pltpu.make_async_copy(whole, out.at[j], sems.at[i, j]))
            made.append(pltpu.make_async_copy(piece, lines.at[i, j], sems.at[2 + i, j]))
        return made

    def start(j, landed):
        for copy in copies(j, landed):
            copy.start()

    for j in range(slots):
        pl.when(plans[j][0])(functools.partial(start, j, True))
        pl.when(jnp.logical_not(plans[j][0]))(functools.partial(start, j, False))
    for j in range(slots):
        _, block, line, alive = plans[j]
        for copy in copies(j, False):
            copy.wait()
        here = lax.broadcasted_iota(jnp.int32, (TILE, HD), 0) == jnp.where(alive, line, -1)
        for i, (fresh, out) in enumerate(((nk, keys), (nv, values))):
            for k in range(KVH):
                columns = slice(k * HD, (k + 1) * HD)
                old = lines[i, j, :, columns].astype(jnp.float32)
                new = fresh[k, j : j + 1].astype(jnp.float32)
                lines[i, j, :, columns] = jnp.where(here, new, old).astype(jnp.bfloat16)
            pltpu.make_async_copy(lines.at[i, j], out.at[j, block], sems.at[i, j]).start()
    for j in range(slots):
        for i, out in enumerate((keys, values)):
            pltpu.make_async_copy(lines.at[i, j], out.at[j, plans[j][1]], sems.at[i, j]).wait()


def per_device(
    cache_keys, cache_values, lengths, unfinished, send_slot, send_to, receive_from, land_slot, land_length,
    queries, new_keys, new_values, norm_gain, gate_weight, up_weight, down_weight
):
    chips, n = lax.axis_size("chip"), lax.axis_size(GROUP)
    slots, capacity, kv_width = cache_keys.shape
    if capacity != TILE * n:
        return per_device_small_pieces(
            cache_keys, cache_values, lengths, unfinished, send_slot, send_to, receive_from, land_slot, land_length,
            queries, new_keys, new_values, norm_gain, gate_weight, up_weight, down_weight
        )
    width = queries.shape[1]
    bf16 = jnp.bfloat16
    dma = pltpu.SemaphoreType.DMA
    pieces = (slots, n, TILE, kv_width)

    def by_head(x):
        return x.reshape(slots, -1, HD).transpose(1, 0, 2)

    q, nk, nv = by_head(queries), by_head(new_keys), by_head(new_values)
    lines = HQ + 4 * KVH
    packets, leaving = pl.pallas_call(
        pack_kernel,
        out_shape=(
            jax.ShapeDtypeStruct((n, lines, HD), bf16),
            jax.ShapeDtypeStruct((n, 2 * TILE, kv_width), bf16),
        ),
        in_specs=[spec(SMEM)] * 2 + [spec(VMEM)] * 3 + [spec(pl.ANY)] * 2,
        out_specs=(spec(VMEM), spec(pl.ANY)),
        scratch_shapes=[VMEM((lines, HD), jnp.float32), dma((2,))],
        cost_estimate=cost(0, 2**20),
        name="pack",
    )(send_slot, land_slot, q, nk, nv, cache_keys.reshape(pieces), cache_values.reshape(pieces))
    packets = exchange(packets, GROUP)
    spread = exchange(leaving, GROUP)
    rows = pl.pallas_call(
        attend_kernel,
        out_shape=jax.ShapeDtypeStruct((chips, slots, width), bf16),
        in_specs=[spec(SMEM)] * 4 + [spec(VMEM)] * 5 + [spec(pl.ANY)] * 2,
        out_specs=spec(VMEM),
        scratch_shapes=[
            VMEM(cache_keys.shape, bf16),
            VMEM(cache_keys.shape, bf16),
            VMEM((HQ, slots, HD), jnp.float32),
            VMEM((HQ, slots, HD), jnp.float32),
            dma((2, slots)),
        ],
        compiler_params=pltpu.CompilerParams(vmem_limit_bytes=24 * 2**20),
        cost_estimate=cost(2**24, 2**21),
        name="attend",
    )(
        send_slot, send_to, lengths, unfinished, packets, q, nk, nv, norm_gain.reshape(HQ, HD), cache_keys, cache_values
    )
    by_chip = exchange(rows, "chip")
    chosen, pick = pl.pallas_call(
        select_kernel,
        out_shape=(
            jax.ShapeDtypeStruct((n, 2 * TILE, kv_width), bf16),
            jax.ShapeDtypeStruct((n * slots, n * slots), bf16),
        ),
        in_specs=[spec(SMEM)] * 4 + [spec(pl.ANY)] * 2,
        out_specs=(spec(pl.ANY), spec(VMEM)),
        scratch_shapes=[dma((n,))],
        cost_estimate=cost(0, 2**20),
        name="select",
    )(send_slot, send_to, receive_from, land_slot, spread, rows)
    arrived = exchange(chosen, GROUP)
    other = lax.ppermute(by_chip, "core", [(0, 1), (1, 0)])
    gathered = jnp.concatenate([by_chip, other], axis=0).reshape(n * slots, width)
    gate = jnp.dot(gathered, gate_weight, preferred_element_type=jnp.float32)
    up_part = jnp.dot(gathered, up_weight, preferred_element_type=jnp.float32)
    hidden = (jax.nn.silu(gate) * up_part).astype(bf16)
    placed_hidden = jnp.dot(pick, hidden, preferred_element_type=jnp.float32).astype(bf16)
    partial = jnp.dot(placed_hidden, down_weight, preferred_element_type=jnp.float32)
    half = chips * slots
    from_other = lax.ppermute(partial[:half].astype(bf16), "core", [(0, 1), (1, 0)])
    chip_sum = (partial[half:] + from_other.astype(jnp.float32)).astype(bf16).reshape(chips, slots, width)
    summed = exchange(chip_sum, "chip")
    decoded = jnp.sum(summed.astype(jnp.float32), axis=0).astype(bf16)
    keys_after, values_after = pl.pallas_call(
        merge_kernel,
        out_shape=(jax.ShapeDtypeStruct(pieces, bf16), jax.ShapeDtypeStruct(pieces, bf16)),
        in_specs=[spec(SMEM)] * 7 + [spec(VMEM)] * 2 + [spec(pl.ANY)] * 4,
        out_specs=(spec(pl.ANY), spec(pl.ANY)),
        scratch_shapes=[VMEM((2, slots, TILE, kv_width), bf16), dma((4, slots))],
        cost_estimate=cost(0, 2**23),
        name="merge",
    )(
        send_slot, send_to, receive_from, land_slot, land_length, lengths, unfinished, nk, nv,
        cache_keys.reshape(pieces), cache_values.reshape(pieces), arrived, chip_sum
    )
    return (decoded, keys_after.reshape(cache_keys.shape), values_after.reshape(cache_keys.shape))


def per_device_small_pieces(
    cache_keys,
    cache_values,
    lengths,
    unfinished,
    send_slot,
    send_to,
    receive_from,
    land_slot,
    land_length,
    queries,
    new_keys,
    new_values,
    norm_gain,
    gate_weight,
    up_weight,
    down_weight,
):
    group = GROUP
    me = lax.axis_index(group)
    chips, n = lax.axis_size("chip"), lax.axis_size(group)
    my_chip, my_core = lax.axis_index("chip"), lax.axis_index("core")
    slots, capacity, kv_width = cache_keys.shape
    width = queries.shape[1]
    slot_ids = jnp.arange(slots)
    target, source = send_to[me], receive_from[me]
    given_slot, taken_slot = send_slot[me], land_slot[me]
    giving, arriving = target != me, source != me
    landing = (slot_ids == taken_slot) & arriving
    vacated = (slot_ids == given_slot) & giving

    packet = jnp.concatenate(
        [
            lax.dynamic_index_in_dim(queries, taken_slot, 0, keepdims=False),
            lax.dynamic_index_in_dim(new_keys, taken_slot, 0, keepdims=False),
            lax.dynamic_index_in_dim(new_values, taken_slot, 0, keepdims=False),
        ]
    ).reshape(-1, 128)
    packets = exchange(jnp.broadcast_to(packet[None], (n,) + packet.shape), group)
    got = lax.dynamic_index_in_dim(packets, target, 0, keepdims=False).reshape(-1)

    rows = capacity // n
    leaving = jnp.concatenate(
        [
            lax.dynamic_index_in_dim(cache_keys, given_slot, 0, keepdims=False).reshape(n, rows, kv_width),
            lax.dynamic_index_in_dim(cache_values, given_slot, 0, keepdims=False).reshape(n, rows, kv_width),
        ],
        axis=1,
    )
    spread = exchange(leaving, group)

    row_queries = jnp.where(vacated[:, None], got[None, :width], queries)
    row_keys = jnp.where(vacated[:, None], got[None, width : width + kv_width], new_keys)
    row_values = jnp.where(vacated[:, None], got[None, width + kv_width :], new_values)
    row_alive = jnp.where(vacated, 1, jnp.where(landing, 0, unfinished)) > 0
    positions = jnp.arange(capacity)
    append = (positions[None, :] == lengths[:, None]) & row_alive[:, None]
    keys_here = jnp.where(append[:, :, None], row_keys[:, None, :], cache_keys)
    values_here = jnp.where(append[:, :, None], row_values[:, None, :], cache_values)
    query_heads = row_queries.reshape(slots, KVH, HQ // KVH, HD)
    key_heads = keys_here.reshape(slots, capacity, KVH, HD)
    value_heads = values_here.reshape(slots, capacity, KVH, HD)
    scores = jnp.einsum(
        "skgd,sckd->skgc", query_heads, key_heads, preferred_element_type=jnp.float32
    ) * (1.0 / math.sqrt(HD))
    visible = (positions[None, :] <= lengths[:, None])[:, None, None, :]
    scores = jnp.where(visible, scores, jnp.float32(-1e30))
    top = jnp.max(scores, axis=-1, keepdims=True)
    expo = jnp.exp(scores - top)
    probs = (expo / jnp.sum(expo, axis=-1, keepdims=True)).astype(jnp.bfloat16)
    attended = jnp.einsum(
        "skgc,sckd->skgd", probs, value_heads, preferred_element_type=jnp.float32
    ).reshape(slots, HQ * HD)
    mean_square = jnp.mean(attended * attended, axis=-1, keepdims=True)
    normed = attended * lax.rsqrt(mean_square + 1e-06) * norm_gain[None, :]
    normed = jnp.where(row_alive[:, None], normed, 0.0).astype(jnp.bfloat16)

    by_chip = exchange(jnp.broadcast_to(normed[None], (chips,) + normed.shape), "chip")
    other = lax.ppermute(by_chip, "core", [(0, 1), (1, 0)])

    chosen = jnp.take(spread, jnp.clip(receive_from, 0, n - 1), axis=0)
    arrived = exchange(chosen, group)
    arrived_keys = arrived[:, :rows].reshape(capacity, kv_width)
    arrived_values = arrived[:, rows:].reshape(capacity, kv_width)
    length_now = jnp.where(landing, land_length[me], lengths)
    alive = jnp.where(vacated, 0, jnp.where(landing, 1, unfinished)) > 0
    append_now = (positions[None, :] == length_now[:, None]) & alive[:, None]
    keys_after = jnp.where(landing[:, None, None], arrived_keys[None], cache_keys)
    values_after = jnp.where(landing[:, None, None], arrived_values[None], cache_values)
    keys_after = jnp.where(append_now[:, :, None], new_keys[:, None, :], keys_after)
    values_after = jnp.where(append_now[:, :, None], new_values[:, None, :], values_after)

    gathered = jnp.concatenate([by_chip, other], axis=0).reshape(n * slots, width)
    gate = jnp.dot(gathered, gate_weight, preferred_element_type=jnp.float32)
    up_part = jnp.dot(gathered, up_weight, preferred_element_type=jnp.float32)
    hidden = (jax.nn.silu(gate) * up_part).astype(jnp.bfloat16)
    everyone = jnp.arange(n)
    arrives = receive_from != everyone
    gives = send_to != everyone
    row_of = everyone[:, None] * slots + slot_ids[None, :]
    from_row = jnp.where(
        arrives[:, None] & (slot_ids[None, :] == land_slot[:, None]),
        (receive_from * slots + jnp.take(send_slot, jnp.clip(receive_from, 0, n - 1)))[:, None],
        row_of,
    )
    from_row = jnp.where(gives[:, None] & (slot_ids[None, :] == send_slot[:, None]), -1, from_row)
    order = jnp.concatenate([jnp.arange(chips) * 2 + 1 - my_core, jnp.arange(chips) * 2 + my_core])
    held = jnp.concatenate([jnp.arange(chips) * 2 + my_core, jnp.arange(chips) * 2 + 1 - my_core])
    wanted = jnp.take(from_row, order, axis=0).reshape(-1)
    held_row = (held[:, None] * slots + slot_ids[None, :]).reshape(-1)
    pick = (wanted[:, None] == held_row[None, :]).astype(jnp.bfloat16)
    placed_hidden = jnp.dot(pick, hidden, preferred_element_type=jnp.float32).astype(jnp.bfloat16)
    partial = jnp.dot(placed_hidden, down_weight, preferred_element_type=jnp.float32)
    half = chips * slots
    from_other = lax.ppermute(partial[:half].astype(jnp.bfloat16), "core", [(0, 1), (1, 0)])
    chip_sum = (partial[half:] + from_other.astype(jnp.float32)).astype(jnp.bfloat16)
    pieces = exchange(chip_sum.reshape(chips, slots, width), "chip")
    decoded = jnp.sum(pieces.astype(jnp.float32), axis=0).astype(jnp.bfloat16)
    return (decoded, keys_after, values_after)


def solution(mesh):
    parts, n = mesh.shape["parts"], mesh.shape["dp"]
    split = jax.sharding.Mesh(mesh.devices.reshape(parts, n // 2, 2), ("parts", "chip", "core"))
    every, own = ("parts", "chip", "core"), ("chip", "core")
    placed = (
        P(every, None, None),
        P(every, None, None),
        P(every),
        P(every),
        P("parts"),
        P("parts"),
        P("parts"),
        P("parts"),
        P("parts"),
        P(every, None),
        P(every, None),
        P(every, None),
        P(),
        P(None, own),
        P(None, own),
        P(own, None),
    )
    return jax.shard_map(
        per_device,
        mesh=split,
        in_specs=placed,
        out_specs=(P(every, None), P(every, None, None), P(every, None, None)),
        check_vma=False,
    )
```

```python
import math

import jax
import jax.numpy as jnp
from jax import lax
from jax.experimental import pallas as pl
from jax.experimental.pallas import tpu as pltpu
from jax.sharding import PartitionSpec as P

HQ = 32
KVH = 4
HD = 128
PER = HQ // KVH
TILE = 16
GROUP = ("chip", "core")
SMEM, VMEM = pltpu.SMEM, pltpu.VMEM


def exchange(blocks, axis):
    return lax.all_to_all(blocks, axis, 0, 0, tiled=True)


def spec(space):
    return pl.BlockSpec(memory_space=space)


def cost(flops, moved):
    return pl.CostEstimate(flops=flops, bytes_accessed=moved, transcendentals=0)


def pack_kernel(send_slot, send_to, receive_from, land_slot, q, nk, nv, ck, cv, leaving, packet, sems):
    me = lax.axis_index(GROUP)
    slots = q.shape[1]
    giving = send_to[me] != me
    copies = [
        pltpu.make_async_copy(cache.at[send_slot[me]], leaving.at[:, pl.ds(i * TILE, TILE)], sems.at[i])
        for i, cache in enumerate((ck, cv))
    ]

    @pl.when(giving)
    def _():
        for copy in copies:
            copy.start()
        for copy in copies:
            copy.wait()

    @pl.when(jnp.logical_not(giving))
    def _():
        taken = land_slot[me]

        def line(x):
            mine = lax.broadcasted_iota(jnp.int32, (x.shape[0], slots, HD), 1) == taken
            return jnp.sum(jnp.where(mine, x[...].astype(jnp.float32), 0.0), axis=1)

        heads, key, value = line(q), line(nk), line(nv)
        packet[...] = jnp.zeros_like(packet)
        for k in range(KVH):
            columns = slice(k * HD, (k + 1) * HD)
            packet[0:PER, columns] = heads[k * PER : (k + 1) * PER]
            packet[PER : PER + 1, columns] = key[k : k + 1]
            packet[PER + 1 : PER + 2, columns] = value[k : k + 1]
        leaving[receive_from[me], 0:TILE] = packet[...].astype(jnp.bfloat16)


def put_line(buf, at, base, line, fresh):
    here = lax.broadcasted_iota(jnp.int32, (TILE, HD), 0) == line
    for k in range(KVH):
        columns = slice(k * HD, (k + 1) * HD)
        old = buf[at, pl.ds(base, TILE), columns].astype(jnp.float32)
        buf[at, pl.ds(base, TILE), columns] = jnp.where(here, fresh[k], old).astype(jnp.bfloat16)


def attend_kernel(
    send_slot, send_to, lengths, unfinished, q, nk, nv, gain, spread, ck, cv, out,
    kbuf, vbuf, tile, q32, att, sems, tile_sem
):
    me = lax.axis_index(GROUP)
    slots = ck.shape[0]
    target, given = send_to[me], send_slot[me]
    fetch = pltpu.make_async_copy(spread.at[target, pl.ds(0, TILE)], tile, tile_sem)
    fetch.start()
    loads = []
    for j in range(slots):
        loads.append(
            (
                pltpu.make_async_copy(ck.at[j], kbuf.at[j], sems.at[0, j]),
                pltpu.make_async_copy(cv.at[j], vbuf.at[j], sems.at[1, j]),
            )
        )
        for copy in loads[j]:
            copy.start()
    q32[...] = q[...].astype(jnp.float32)
    nk32, nv32 = nk[...].astype(jnp.float32), nv[...].astype(jnp.float32)
    fetch.wait()
    packet = tile[...].astype(jnp.float32)
    scale = 1.0 / math.sqrt(HD)
    for j in range(slots):
        moved = (target != me) & (given == j)
        alive = jnp.where(moved, 1, unfinished[j]) > 0
        length = lengths[j]
        block = length // TILE
        base = pl.multiple_of(block * TILE, TILE)
        line = jnp.where(alive, length - block * TILE, -1)

        def fresh(row, own):
            return [
                jnp.where(moved, packet[row : row + 1, k * HD : (k + 1) * HD], own[k, j : j + 1]) for k in range(KVH)
            ]

        for copy in loads[j]:
            copy.wait()
        put_line(kbuf, j, base, line, fresh(PER, nk32))
        put_line(vbuf, j, base, line, fresh(PER + 1, nv32))
        own_heads = q32[:, j, :]
        scores = jnp.concatenate(
            [
                lax.dot_general(
                    jnp.where(moved, packet[0:PER, k * HD : (k + 1) * HD], own_heads[k * PER : (k + 1) * PER]).astype(
                        jnp.bfloat16
                    ),
                    kbuf[j, :, k * HD : (k + 1) * HD],
                    (((1,), (1,)), ((), ())),
                    preferred_element_type=jnp.float32,
                )
                for k in range(KVH)
            ],
            axis=0,
        )
        visible = lax.broadcasted_iota(jnp.int32, scores.shape, 1) <= length
        scores = jnp.where(visible, scores * scale, jnp.float32(-1e30))
        expo = jnp.exp(scores - jnp.max(scores, axis=1, keepdims=True))
        probs = expo / jnp.sum(expo, axis=1, keepdims=True)
        attended = jnp.concatenate(
            [
                jnp.dot(
                    probs[k * PER : (k + 1) * PER].astype(jnp.bfloat16),
                    vbuf[j, :, k * HD : (k + 1) * HD],
                    preferred_element_type=jnp.float32,
                )
                for k in range(KVH)
            ],
            axis=0,
        )
        mean = jnp.sum(attended * attended, keepdims=True) * (1.0 / (HQ * HD))
        normed = attended * lax.rsqrt(mean + 1e-06) * gain[...]
        att[:, j, :] = jnp.where(alive, normed, 0.0)
    for h in range(HQ):
        head = att[h].astype(jnp.bfloat16)
        for c in range(out.shape[0]):
            out[c, :, h * HD : (h + 1) * HD] = head


def aside_kernel(
    send_slot, send_to, receive_from, land_slot, lengths, unfinished, nk, nv, ck, cv, spread, _,
    keys, values, outgoing, pick, kbuf, vbuf, sems, piece_sem
):
    me = lax.axis_index(GROUP)
    core = lax.axis_index("core")
    slots, n, rows = ck.shape[0], outgoing.shape[0], pick.shape[0]
    half = rows // 2
    pairs = ((ck, kbuf, keys), (cv, vbuf, values))

    def piece(d):
        return pltpu.make_async_copy(spread.at[receive_from[d]], outgoing.at[d, pl.ds(0, 2 * TILE)], piece_sem.at[d])

    def load(i, j):
        return pltpu.make_async_copy(pairs[i][0].at[j], pairs[i][1].at[j], sems.at[i, j])

    def store(i, j):
        return pltpu.make_async_copy(pairs[i][1].at[j], pairs[i][2].at[j], sems.at[i, j])

    for j in range(slots):
        for i in range(2):
            load(i, j).start()
    for d in range(n):
        pl.when(receive_from[d] != d)(lambda d=d: piece(d).start())
    row = lax.broadcasted_iota(jnp.int32, (rows, HD), 0)
    device = row // slots
    wanted = jnp.where((device & 1) == core, 0, half) + (device >> 1) * slots + (row & (slots - 1))
    for d in range(n):
        source = receive_from[d]
        held = jnp.where(lax.rem(source, 2) == core, 0, half) + (source // 2) * slots + send_slot[source]
        landing = jnp.where(source != d, d * slots + land_slot[d], -1)
        vacated = jnp.where(send_to[d] != d, d * slots + send_slot[d], -1)
        wanted = jnp.where(row == landing, held, wanted)
        wanted = jnp.where(row == vacated, -1, wanted)
    column = lax.broadcasted_iota(jnp.int32, (rows, rows), 1)
    pick[...] = (column == wanted[:, :1]).astype(jnp.float32).astype(jnp.bfloat16)
    for j in range(slots):
        vacated = (send_to[me] != me) & (send_slot[me] == j)
        alive = jnp.where(vacated, 0, unfinished[j]) > 0
        length = lengths[j]
        block = length // TILE
        base = pl.multiple_of(block * TILE, TILE)
        line = jnp.where(alive, length - block * TILE, -1)
        for i, own in enumerate((nk, nv)):
            load(i, j).wait()
            put_line(pairs[i][1], j, base, line, [own[k, j : j + 1].astype(jnp.float32) for k in range(KVH)])
            store(i, j).start()
    for d in range(n):
        pl.when(receive_from[d] != d)(lambda d=d: piece(d).wait())
    for j in range(slots):
        for i in range(2):
            store(i, j).wait()


def ffn_kernel(near, far, gate_weight, up_weight, pick, down_weight, mine, theirs):
    core = lax.axis_index("core")
    x = jnp.concatenate([near[...], far[...]], axis=0)
    gate = jnp.dot(x, gate_weight[...], preferred_element_type=jnp.float32)
    up_part = jnp.dot(x, up_weight[...], preferred_element_type=jnp.float32)
    hidden = (gate / (1.0 + jnp.exp(-gate)) * up_part).astype(jnp.bfloat16)
    hidden = jnp.dot(pick[...], hidden, preferred_element_type=jnp.float32).astype(jnp.bfloat16)
    width = mine.shape[1]

    def down(side):
        columns = pl.ds(pl.multiple_of(side * width, width), width)
        return jnp.dot(hidden, down_weight[:, columns], preferred_element_type=jnp.float32)

    theirs[...] = down(1 - core).astype(jnp.bfloat16)
    mine[...] = down(core)


def place_kernel(mine, theirs, outgoing, out, rows, sem):
    n, _, wide = rows.shape
    slots = mine.shape[0] // n
    for d in range(n):
        at = slice(d * slots, (d + 1) * slots)
        both = mine[at] + theirs[at].astype(jnp.float32)
        rows[d] = jnp.concatenate(
            [both[:, g * wide : (g + 1) * wide] for g in range(both.shape[1] // wide)], axis=0
        ).astype(jnp.bfloat16)
    copy = pltpu.make_async_copy(rows, out.at[:, pl.ds(2 * TILE, TILE)], sem)
    copy.start()
    copy.wait()


def finish_kernel(
    receive_from, land_slot, land_length, nk, nv, arrived, keys_in, values_in, decoded, keys, values,
    kbuf, vbuf, sums, sems
):
    me = lax.axis_index(GROUP)
    n, wide = sums.shape[0], sums.shape[2]
    slots, slot = decoded.shape[0], land_slot[me]
    arriving = receive_from[me] != me
    bring = pltpu.make_async_copy(arrived.at[:, pl.ds(2 * TILE, TILE)], sums, sems.at[2])
    bring.start()
    pairs = ((kbuf, keys, nk), (vbuf, values, nv))
    loads = [
        pltpu.make_async_copy(arrived.at[:, pl.ds(i * TILE, TILE)], pairs[i][0].at[0], sems.at[i]) for i in range(2)
    ]
    stores = [pltpu.make_async_copy(pairs[i][0].at[0], pairs[i][1].at[slot], sems.at[i]) for i in range(2)]

    @pl.when(arriving)
    def _():
        for copy in loads:
            copy.start()
        length = land_length[me]
        block = length // TILE
        for i, (buf, _, own) in enumerate(pairs):
            loads[i].wait()
            mine = lax.broadcasted_iota(jnp.int32, (KVH, slots, HD), 1) == slot
            token = jnp.sum(jnp.where(mine, own[...].astype(jnp.float32), 0.0), axis=1)
            here = lax.broadcasted_iota(jnp.int32, (TILE, HD), 0) == length - block * TILE
            for k in range(KVH):
                columns = slice(k * HD, (k + 1) * HD)
                old = buf[0, block, :, columns].astype(jnp.float32)
                buf[0, block, :, columns] = jnp.where(here, token[k : k + 1], old).astype(jnp.bfloat16)
            stores[i].start()

    bring.wait()
    for side in range(2):
        total = sums[side].astype(jnp.float32)
        for c in range(1, n // 2):
            total += sums[2 * c + side].astype(jnp.float32)
        for g in range(TILE // slots):
            at = (side * (TILE // slots) + g) * wide
            decoded[:, at : at + wide] = total[g * slots : (g + 1) * slots].astype(jnp.bfloat16)

    @pl.when(arriving)
    def _():
        for copy in stores:
            copy.wait()


def per_device(
    cache_keys, cache_values, lengths, unfinished, send_slot, send_to, receive_from, land_slot, land_length,
    queries, new_keys, new_values, norm_gain, gate_weight, up_weight, down_weight
):
    chips, n = lax.axis_size("chip"), lax.axis_size(GROUP)
    slots, capacity, kv_width = cache_keys.shape
    width = queries.shape[1]
    if capacity != TILE * n or slots * width != 2 * TILE * kv_width:
        return per_device_small_pieces(
            cache_keys, cache_values, lengths, unfinished, send_slot, send_to, receive_from, land_slot, land_length,
            queries, new_keys, new_values, norm_gain, gate_weight, up_weight, down_weight
        )
    bf16, f32 = jnp.bfloat16, jnp.float32
    dma = pltpu.SemaphoreType.DMA
    pieces = (slots, n, TILE, kv_width)
    room = pltpu.CompilerParams(vmem_limit_bytes=16 * 2**20)

    def shape(dims, kind=bf16):
        return jax.ShapeDtypeStruct(dims, kind)

    def by_head(x):
        return x.reshape(slots, -1, HD).transpose(1, 0, 2)

    q, nk, nv = by_head(queries), by_head(new_keys), by_head(new_values)
    leaving = pl.pallas_call(
        pack_kernel,
        out_shape=shape((n, 2 * TILE, kv_width)),
        in_specs=[spec(SMEM)] * 4 + [spec(VMEM)] * 3 + [spec(pl.ANY)] * 2,
        out_specs=spec(VMEM),
        scratch_shapes=[VMEM((TILE, kv_width), f32), dma((2,))],
        compiler_params=room,
        cost_estimate=cost(0, 2**20),
        name="pack",
    )(
        send_slot, send_to, receive_from, land_slot, q, nk, nv, cache_keys.reshape(pieces), cache_values.reshape(pieces)
    )
    spread = exchange(leaving, GROUP)
    rows = pl.pallas_call(
        attend_kernel,
        out_shape=shape((chips, slots, width)),
        in_specs=[spec(SMEM)] * 4 + [spec(VMEM)] * 4 + [spec(pl.ANY)] * 3,
        out_specs=spec(VMEM),
        scratch_shapes=[
            VMEM(cache_keys.shape, bf16),
            VMEM(cache_keys.shape, bf16),
            VMEM((TILE, kv_width), bf16),
            VMEM((HQ, slots, HD), f32),
            VMEM((HQ, slots, HD), f32),
            dma((2, slots)),
            dma,
        ],
        compiler_params=room,
        cost_estimate=cost(2**24, 2**21),
        name="attend",
    )(
        send_slot, send_to, lengths, unfinished, q, nk, nv, norm_gain.reshape(HQ, HD), spread, cache_keys, cache_values
    )
    near = exchange(rows, "chip")
    keys_own, values_own, outgoing, pick = pl.pallas_call(
        aside_kernel,
        out_shape=(
            shape(cache_keys.shape),
            shape(cache_keys.shape),
            shape((n, 3 * TILE, kv_width)),
            shape((n * slots, n * slots)),
        ),
        in_specs=[spec(SMEM)] * 6 + [spec(VMEM)] * 2 + [spec(pl.ANY)] * 4,
        out_specs=(spec(pl.ANY), spec(pl.ANY), spec(pl.ANY), spec(VMEM)),
        scratch_shapes=[VMEM(cache_keys.shape, bf16), VMEM(cache_keys.shape, bf16), dma((2, slots)), dma((n,))],
        compiler_params=room,
        cost_estimate=cost(0, 2**23),
        name="aside",
    )(
        send_slot, send_to, receive_from, land_slot, lengths, unfinished, nk, nv, cache_keys, cache_values, spread, rows
    )
    near, pick = lax.optimization_barrier((near, pick))
    far = lax.ppermute(near, "core", [(0, 1), (1, 0)])
    mine, theirs = pl.pallas_call(
        ffn_kernel,
        out_shape=(shape((n * slots, width // 2), f32), shape((n * slots, width // 2))),
        in_specs=[spec(VMEM)] * 6,
        out_specs=(spec(VMEM), spec(VMEM)),
        compiler_params=room,
        cost_estimate=cost(6 * n * slots * width * gate_weight.shape[1], 3 * 2**21),
        name="ffn",
    )(
        near.reshape(chips * slots, width), far.reshape(chips * slots, width), gate_weight, up_weight, pick, down_weight
    )
    theirs = lax.ppermute(theirs, "core", [(0, 1), (1, 0)])
    outgoing = pl.pallas_call(
        place_kernel,
        out_shape=shape((n, 3 * TILE, kv_width)),
        in_specs=[spec(VMEM)] * 2 + [spec(pl.ANY)],
        out_specs=spec(pl.ANY),
        scratch_shapes=[VMEM((n, TILE, kv_width), bf16), dma],
        input_output_aliases={2: 0},
        compiler_params=room,
        cost_estimate=cost(0, 2**20),
        name="place",
    )(mine, theirs, outgoing)
    arrived = exchange(outgoing, GROUP)
    decoded, keys_after, values_after = pl.pallas_call(
        finish_kernel,
        out_shape=(shape((slots, width)), shape(pieces), shape(pieces)),
        in_specs=[spec(SMEM)] * 3 + [spec(VMEM)] * 2 + [spec(pl.ANY)] * 3,
        out_specs=(spec(VMEM), spec(pl.ANY), spec(pl.ANY)),
        scratch_shapes=[
            VMEM((1, n, TILE, kv_width), bf16),
            VMEM((1, n, TILE, kv_width), bf16),
            VMEM((n, TILE, kv_width), bf16),
            dma((3,)),
        ],
        input_output_aliases={6: 1, 7: 2},
        compiler_params=room,
        cost_estimate=cost(0, 2**20),
        name="finish",
    )(
        receive_from, land_slot, land_length, nk, nv, arrived, keys_own.reshape(pieces), values_own.reshape(pieces)
    )
    return (decoded, keys_after.reshape(cache_keys.shape), values_after.reshape(cache_keys.shape))


def per_device_small_pieces(
    cache_keys,
    cache_values,
    lengths,
    unfinished,
    send_slot,
    send_to,
    receive_from,
    land_slot,
    land_length,
    queries,
    new_keys,
    new_values,
    norm_gain,
    gate_weight,
    up_weight,
    down_weight,
):
    group = GROUP
    me = lax.axis_index(group)
    chips, n = lax.axis_size("chip"), lax.axis_size(group)
    my_chip, my_core = lax.axis_index("chip"), lax.axis_index("core")
    slots, capacity, kv_width = cache_keys.shape
    width = queries.shape[1]
    slot_ids = jnp.arange(slots)
    target, source = send_to[me], receive_from[me]
    given_slot, taken_slot = send_slot[me], land_slot[me]
    giving, arriving = target != me, source != me
    landing = (slot_ids == taken_slot) & arriving
    vacated = (slot_ids == given_slot) & giving

    packet = jnp.concatenate(
        [
            lax.dynamic_index_in_dim(queries, taken_slot, 0, keepdims=False),
            lax.dynamic_index_in_dim(new_keys, taken_slot, 0, keepdims=False),
            lax.dynamic_index_in_dim(new_values, taken_slot, 0, keepdims=False),
        ]
    ).reshape(-1, 128)
    packets = exchange(jnp.broadcast_to(packet[None], (n,) + packet.shape), group)
    got = lax.dynamic_index_in_dim(packets, target, 0, keepdims=False).reshape(-1)

    rows = capacity // n
    leaving = jnp.concatenate(
        [
            lax.dynamic_index_in_dim(cache_keys, given_slot, 0, keepdims=False).reshape(n, rows, kv_width),
            lax.dynamic_index_in_dim(cache_values, given_slot, 0, keepdims=False).reshape(n, rows, kv_width),
        ],
        axis=1,
    )
    spread = exchange(leaving, group)

    row_queries = jnp.where(vacated[:, None], got[None, :width], queries)
    row_keys = jnp.where(vacated[:, None], got[None, width : width + kv_width], new_keys)
    row_values = jnp.where(vacated[:, None], got[None, width + kv_width :], new_values)
    row_alive = jnp.where(vacated, 1, jnp.where(landing, 0, unfinished)) > 0
    positions = jnp.arange(capacity)
    append = (positions[None, :] == lengths[:, None]) & row_alive[:, None]
    keys_here = jnp.where(append[:, :, None], row_keys[:, None, :], cache_keys)
    values_here = jnp.where(append[:, :, None], row_values[:, None, :], cache_values)
    query_heads = row_queries.reshape(slots, KVH, HQ // KVH, HD)
    key_heads = keys_here.reshape(slots, capacity, KVH, HD)
    value_heads = values_here.reshape(slots, capacity, KVH, HD)
    scores = jnp.einsum(
        "skgd,sckd->skgc", query_heads, key_heads, preferred_element_type=jnp.float32
    ) * (1.0 / math.sqrt(HD))
    visible = (positions[None, :] <= lengths[:, None])[:, None, None, :]
    scores = jnp.where(visible, scores, jnp.float32(-1e30))
    top = jnp.max(scores, axis=-1, keepdims=True)
    expo = jnp.exp(scores - top)
    probs = (expo / jnp.sum(expo, axis=-1, keepdims=True)).astype(jnp.bfloat16)
    attended = jnp.einsum(
        "skgc,sckd->skgd", probs, value_heads, preferred_element_type=jnp.float32
    ).reshape(slots, HQ * HD)
    mean_square = jnp.mean(attended * attended, axis=-1, keepdims=True)
    normed = attended * lax.rsqrt(mean_square + 1e-06) * norm_gain[None, :]
    normed = jnp.where(row_alive[:, None], normed, 0.0).astype(jnp.bfloat16)

    by_chip = exchange(jnp.broadcast_to(normed[None], (chips,) + normed.shape), "chip")
    other = lax.ppermute(by_chip, "core", [(0, 1), (1, 0)])

    chosen = jnp.take(spread, jnp.clip(receive_from, 0, n - 1), axis=0)
    arrived = exchange(chosen, group)
    arrived_keys = arrived[:, :rows].reshape(capacity, kv_width)
    arrived_values = arrived[:, rows:].reshape(capacity, kv_width)
    length_now = jnp.where(landing, land_length[me], lengths)
    alive = jnp.where(vacated, 0, jnp.where(landing, 1, unfinished)) > 0
    append_now = (positions[None, :] == length_now[:, None]) & alive[:, None]
    keys_after = jnp.where(landing[:, None, None], arrived_keys[None], cache_keys)
    values_after = jnp.where(landing[:, None, None], arrived_values[None], cache_values)
    keys_after = jnp.where(append_now[:, :, None], new_keys[:, None, :], keys_after)
    values_after = jnp.where(append_now[:, :, None], new_values[:, None, :], values_after)

    gathered = jnp.concatenate([by_chip, other], axis=0).reshape(n * slots, width)
    gate = jnp.dot(gathered, gate_weight, preferred_element_type=jnp.float32)
    up_part = jnp.dot(gathered, up_weight, preferred_element_type=jnp.float32)
    hidden = (jax.nn.silu(gate) * up_part).astype(jnp.bfloat16)
    everyone = jnp.arange(n)
    arrives = receive_from != everyone
    gives = send_to != everyone
    row_of = everyone[:, None] * slots + slot_ids[None, :]
    from_row = jnp.where(
        arrives[:, None] & (slot_ids[None, :] == land_slot[:, None]),
        (receive_from * slots + jnp.take(send_slot, jnp.clip(receive_from, 0, n - 1)))[:, None],
        row_of,
    )
    from_row = jnp.where(gives[:, None] & (slot_ids[None, :] == send_slot[:, None]), -1, from_row)
    order = jnp.concatenate([jnp.arange(chips) * 2 + 1 - my_core, jnp.arange(chips) * 2 + my_core])
    held = jnp.concatenate([jnp.arange(chips) * 2 + my_core, jnp.arange(chips) * 2 + 1 - my_core])
    wanted = jnp.take(from_row, order, axis=0).reshape(-1)
    held_row = (held[:, None] * slots + slot_ids[None, :]).reshape(-1)
    pick = (wanted[:, None] == held_row[None, :]).astype(jnp.bfloat16)
    placed_hidden = jnp.dot(pick, hidden, preferred_element_type=jnp.float32).astype(jnp.bfloat16)
    partial = jnp.dot(placed_hidden, down_weight, preferred_element_type=jnp.float32)
    half = chips * slots
    from_other = lax.ppermute(partial[:half].astype(jnp.bfloat16), "core", [(0, 1), (1, 0)])
    chip_sum = (partial[half:] + from_other.astype(jnp.float32)).astype(jnp.bfloat16)
    pieces = exchange(chip_sum.reshape(chips, slots, width), "chip")
    decoded = jnp.sum(pieces.astype(jnp.float32), axis=0).astype(jnp.bfloat16)
    return (decoded, keys_after, values_after)


def solution(mesh):
    parts, n = mesh.shape["parts"], mesh.shape["dp"]
    split = jax.sharding.Mesh(mesh.devices.reshape(parts, n // 2, 2), ("parts", "chip", "core"))
    every, own = ("parts", "chip", "core"), ("chip", "core")
    placed = (
        P(every, None, None),
        P(every, None, None),
        P(every),
        P(every),
        P("parts"),
        P("parts"),
        P("parts"),
        P("parts"),
        P("parts"),
        P(every, None),
        P(every, None),
        P(every, None),
        P(),
        P(None, own),
        P(None, own),
        P(own, None),
    )
    return jax.shard_map(
        per_device,
        mesh=split,
        in_specs=placed,
        out_specs=(P(every, None), P(every, None, None), P(every, None, None)),
        check_vma=False,
    )
```

```python
import math

import jax
import jax.numpy as jnp
from jax import lax
from jax.experimental import pallas as pl
from jax.experimental.pallas import tpu as pltpu
from jax.sharding import PartitionSpec as P

HQ = 32
KVH = 4
HD = 128
PER = HQ // KVH
TILE = 16
CHUNKS = 4
GROUP = ("chip", "core")
SMEM, VMEM = pltpu.SMEM, pltpu.VMEM


def exchange(blocks, axis):
    return lax.all_to_all(blocks, axis, 0, 0, tiled=True)


def spec(space):
    return pl.BlockSpec(memory_space=space)


def cost(flops, moved):
    return pl.CostEstimate(flops=flops, bytes_accessed=moved, transcendentals=0)


def pack_kernel(
    send_slot, send_to, receive_from, land_slot, q, nk, nv, ck, cv, leaving,
    slot_s, to_s, from_s, land_s, qb, kb, vb, packet, sems
):
    me = lax.axis_index(GROUP)
    slots = q.shape[1]
    fetches = [
        pltpu.make_async_copy(a, b, sems.at[2 + i])
        for i, (a, b) in enumerate(
            (
                (send_slot, slot_s), (send_to, to_s), (receive_from, from_s), (land_slot, land_s),
                (q, qb), (nk, kb), (nv, vb),
            )
        )
    ]
    for fetch in fetches:
        fetch.start()
    for fetch in fetches[:4]:
        fetch.wait()
    giving = to_s[me] != me
    copies = [
        pltpu.make_async_copy(cache.at[slot_s[me]], leaving.at[:, pl.ds(i * TILE, TILE)], sems.at[i])
        for i, cache in enumerate((ck, cv))
    ]

    @pl.when(giving)
    def _():
        for copy in copies:
            copy.start()

    for fetch in fetches[4:]:
        fetch.wait()

    @pl.when(giving)
    def _():
        for copy in copies:
            copy.wait()

    @pl.when(jnp.logical_not(giving))
    def _():
        taken = land_s[me]

        def line(x):
            mine = lax.broadcasted_iota(jnp.int32, (x.shape[0], slots, HD), 1) == taken
            return jnp.sum(jnp.where(mine, x[...].astype(jnp.float32), 0.0), axis=1)

        heads, key, value = line(qb), line(kb), line(vb)
        packet[...] = jnp.zeros_like(packet)
        for k in range(KVH):
            columns = slice(k * HD, (k + 1) * HD)
            packet[0:PER, columns] = heads[k * PER : (k + 1) * PER]
            packet[PER : PER + 1, columns] = key[k : k + 1]
            packet[PER + 1 : PER + 2, columns] = value[k : k + 1]
        leaving[from_s[me], 0:TILE] = packet[...].astype(jnp.bfloat16)


def put_line(buf, at, base, line, fresh):
    here = lax.broadcasted_iota(jnp.int32, (TILE, HD), 0) == line
    for k in range(KVH):
        columns = slice(k * HD, (k + 1) * HD)
        old = buf[at, pl.ds(base, TILE), columns].astype(jnp.float32)
        buf[at, pl.ds(base, TILE), columns] = jnp.where(here, fresh[k], old).astype(jnp.bfloat16)


def place_of(length, alive):
    block = length // TILE
    return pl.multiple_of(block * TILE, TILE), jnp.where(alive, length - block * TILE, -1)


def attend(heads, kbuf, vbuf, at, length, gain):
    scores = jnp.concatenate(
        [
            lax.dot_general(
                heads[k].astype(jnp.bfloat16),
                kbuf[at, :, k * HD : (k + 1) * HD],
                (((1,), (1,)), ((), ())),
                preferred_element_type=jnp.float32,
            )
            for k in range(KVH)
        ],
        axis=0,
    )
    visible = lax.broadcasted_iota(jnp.int32, scores.shape, 1) <= length
    scores = jnp.where(visible, scores * (1.0 / math.sqrt(HD)), jnp.float32(-1e30))
    expo = jnp.exp(scores - jnp.max(scores, axis=1, keepdims=True))
    probs = expo / jnp.sum(expo, axis=1, keepdims=True)
    attended = jnp.concatenate(
        [
            jnp.dot(
                probs[k * PER : (k + 1) * PER].astype(jnp.bfloat16),
                vbuf[at, :, k * HD : (k + 1) * HD],
                preferred_element_type=jnp.float32,
            )
            for k in range(KVH)
        ],
        axis=0,
    )
    mean = jnp.sum(attended * attended, keepdims=True) * (1.0 / (HQ * HD))
    return attended * lax.rsqrt(mean + 1e-06) * gain


def local_kernel(
    send_slot, send_to, receive_from, land_slot, lengths, unfinished, q, nk, nv, gain, ck, cv,
    att, keys, values, given_row, pick,
    slot_s, to_s, from_s, land_s, length_s, left_s, qb, kb, vb, gb, q32, kbuf, vbuf, sems, small, big
):
    me = lax.axis_index(GROUP)
    core = lax.axis_index("core")
    slots, n, rows = ck.shape[0], slot_s.shape[0], pick.shape[0]
    half = rows // 2
    pairs = ((ck, kbuf, keys), (cv, vbuf, values))
    fetches = [
        pltpu.make_async_copy(a, b, small.at[i])
        for i, (a, b) in enumerate(
            (
                (send_slot, slot_s), (send_to, to_s), (receive_from, from_s), (land_slot, land_s),
                (lengths, length_s), (unfinished, left_s), (q, qb), (nk, kb), (nv, vb), (gain, gb),
            )
        )
    ]
    for fetch in fetches:
        fetch.start()

    def load(i, j):
        return pltpu.make_async_copy(pairs[i][0].at[j], pairs[i][1].at[j], sems.at[i, j])

    def store(i, j):
        return pltpu.make_async_copy(pairs[i][1].at[j], pairs[i][2].at[j], sems.at[i, j])

    for j in range(slots):
        for i in range(2):
            load(i, j).start()
    for fetch in fetches:
        fetch.wait()
    large = [pltpu.make_async_copy(pairs[i][0].at[slot_s[me]], given_row.at[i], big.at[i]) for i in range(2)]
    for copy in large:
        copy.start()
    row = lax.broadcasted_iota(jnp.int32, (rows, HD), 0)
    device = row // slots
    wanted = jnp.where((device & 1) == core, 0, half) + (device >> 1) * slots + (row & (slots - 1))
    for d in range(n):
        source = from_s[d]
        held = jnp.where(lax.rem(source, 2) == core, 0, half) + (source // 2) * slots + slot_s[source]
        landing = jnp.where(source != d, d * slots + land_s[d], -1)
        vacated = jnp.where(to_s[d] != d, d * slots + slot_s[d], -1)
        wanted = jnp.where(row == landing, held, wanted)
        wanted = jnp.where(row == vacated, -1, wanted)
    column = lax.broadcasted_iota(jnp.int32, (rows, rows), 1)
    pick[...] = (column == wanted[:, :1]).astype(jnp.float32).astype(jnp.bfloat16)
    q32[...] = qb[...].astype(jnp.float32)
    for j in range(slots):
        vacated = (to_s[me] != me) & (slot_s[me] == j)
        alive = jnp.where(vacated, 0, left_s[j]) > 0
        length = length_s[j]
        base, line = place_of(length, alive)
        for i, own in enumerate((kb, vb)):
            load(i, j).wait()
            put_line(pairs[i][1], j, base, line, [own[k, j : j + 1].astype(jnp.float32) for k in range(KVH)])
            store(i, j).start()
        own_heads = q32[:, j, :]
        normed = attend([own_heads[k * PER : (k + 1) * PER] for k in range(KVH)], kbuf, vbuf, j, length, gb[...])
        att[:, j, :] = jnp.where(alive, normed, 0.0)
    for j in range(slots):
        for i in range(2):
            store(i, j).wait()
    for copy in large:
        copy.wait()


def moved_kernel(send_slot, send_to, lengths, gain, att, given_row, spread, out, mine, kv, tile, sem):
    me = lax.axis_index(GROUP)
    mine[...] = att[...]

    @pl.when(send_to[me] != me)
    def _():
        fetch = pltpu.make_async_copy(spread.at[send_to[me], pl.ds(0, TILE)], tile, sem)
        fetch.start()
        kv[...] = given_row[...]
        slots = mine.shape[1]
        given = send_slot[me]
        length = lengths[given]
        base, line = place_of(length, True)
        fetch.wait()
        packet = tile[...].astype(jnp.float32)
        for i in range(2):
            put_line(kv, i, base, line, [packet[PER + i : PER + i + 1, k * HD : (k + 1) * HD] for k in range(KVH)])
        heads = [packet[0:PER, k * HD : (k + 1) * HD] for k in range(KVH)]
        normed = attend(heads, kv.at[0:1], kv.at[1:2], 0, length, gain[...])
        for j in range(slots):
            pl.when(given == j)(lambda j=j: mine.__setitem__((slice(None), j, slice(None)), normed))

    for h in range(HQ):
        head = mine[h].astype(jnp.bfloat16)
        for c in range(out.shape[0]):
            out[c, :, h * HD : (h + 1) * HD] = head


def select_kernel(receive_from, spread, _, outgoing, piece_sem):
    n = outgoing.shape[0]

    def piece(d):
        return pltpu.make_async_copy(spread.at[receive_from[d]], outgoing.at[d, pl.ds(0, 2 * TILE)], piece_sem.at[d])

    for d in range(n):
        pl.when(receive_from[d] != d)(lambda d=d: piece(d).start())
    for d in range(n):
        pl.when(receive_from[d] != d)(lambda d=d: piece(d).wait())


def ffn_kernel(near, far, pick, gate_weight, up_weight, down_weight, mine, theirs, gate_v, up_v, down_v, sems):
    core = lax.axis_index("core")
    width = mine.shape[1]
    step = gate_v.shape[0] // CHUNKS
    sides = [pl.ds(pl.multiple_of(side * width, width), width) for side in (1 - core, core)]
    loads = []
    for c in range(CHUNKS):
        at = pl.ds(c * step, step)
        loads.append(pltpu.make_async_copy(gate_weight.at[at], gate_v.at[at], sems.at[0, c]))
        loads.append(pltpu.make_async_copy(up_weight.at[at], up_v.at[at], sems.at[1, c]))
    downs = [pltpu.make_async_copy(down_weight.at[:, at], down_v.at[:, at], sems.at[2, i]) for i, at in enumerate(sides)]
    for load in loads + downs:
        load.start()
    gate = up_part = 0.0
    for c in range(CHUNKS):
        at = slice(c * step, (c + 1) * step)
        x = jnp.concatenate([near[:, at], far[:, at]], axis=0)
        loads[2 * c].wait()
        gate += jnp.dot(x, gate_v[at], preferred_element_type=jnp.float32)
        loads[2 * c + 1].wait()
        up_part += jnp.dot(x, up_v[at], preferred_element_type=jnp.float32)
    hidden = (gate / (1.0 + jnp.exp(-gate)) * up_part).astype(jnp.bfloat16)
    hidden = jnp.dot(pick[...], hidden, preferred_element_type=jnp.float32).astype(jnp.bfloat16)
    downs[0].wait()
    theirs[...] = jnp.dot(hidden, down_v[:, sides[0]], preferred_element_type=jnp.float32).astype(jnp.bfloat16)
    downs[1].wait()
    mine[...] = jnp.dot(hidden, down_v[:, sides[1]], preferred_element_type=jnp.float32)


def place_kernel(mine, theirs, outgoing, out, rows, sem):
    n, _, wide = rows.shape
    slots = mine.shape[0] // n
    for d in range(n):
        at = slice(d * slots, (d + 1) * slots)
        both = mine[at] + theirs[at].astype(jnp.float32)
        rows[d] = jnp.concatenate(
            [both[:, g * wide : (g + 1) * wide] for g in range(both.shape[1] // wide)], axis=0
        ).astype(jnp.bfloat16)
    copy = pltpu.make_async_copy(rows, out.at[:, pl.ds(2 * TILE, TILE)], sem)
    copy.start()
    copy.wait()


def finish_kernel(
    receive_from, land_slot, land_length, nk, nv, arrived, keys_in, values_in, decoded, keys, values,
    kbuf, vbuf, sums, sems
):
    me = lax.axis_index(GROUP)
    n, wide = sums.shape[0], sums.shape[2]
    slots, slot = decoded.shape[0], land_slot[me]
    arriving = receive_from[me] != me
    bring = pltpu.make_async_copy(arrived.at[:, pl.ds(2 * TILE, TILE)], sums, sems.at[2])
    bring.start()
    pairs = ((kbuf, keys, nk), (vbuf, values, nv))
    loads = [
        pltpu.make_async_copy(arrived.at[:, pl.ds(i * TILE, TILE)], pairs[i][0].at[0], sems.at[i]) for i in range(2)
    ]
    stores = [pltpu.make_async_copy(pairs[i][0].at[0], pairs[i][1].at[slot], sems.at[i]) for i in range(2)]

    @pl.when(arriving)
    def _():
        for copy in loads:
            copy.start()
        length = land_length[me]
        block = length // TILE
        for i, (buf, _, own) in enumerate(pairs):
            loads[i].wait()
            mine = lax.broadcasted_iota(jnp.int32, (KVH, slots, HD), 1) == slot
            token = jnp.sum(jnp.where(mine, own[...].astype(jnp.float32), 0.0), axis=1)
            here = lax.broadcasted_iota(jnp.int32, (TILE, HD), 0) == length - block * TILE
            for k in range(KVH):
                columns = slice(k * HD, (k + 1) * HD)
                old = buf[0, block, :, columns].astype(jnp.float32)
                buf[0, block, :, columns] = jnp.where(here, token[k : k + 1], old).astype(jnp.bfloat16)
            stores[i].start()

    bring.wait()
    for side in range(2):
        total = sums[side].astype(jnp.float32)
        for c in range(1, n // 2):
            total += sums[2 * c + side].astype(jnp.float32)
        for g in range(TILE // slots):
            at = (side * (TILE // slots) + g) * wide
            decoded[:, at : at + wide] = total[g * slots : (g + 1) * slots].astype(jnp.bfloat16)

    @pl.when(arriving)
    def _():
        for copy in stores:
            copy.wait()


def per_device(
    cache_keys, cache_values, lengths, unfinished, send_slot, send_to, receive_from, land_slot, land_length,
    queries, new_keys, new_values, norm_gain, gate_weight, up_weight, down_weight
):
    chips, n = lax.axis_size("chip"), lax.axis_size(GROUP)
    slots, capacity, kv_width = cache_keys.shape
    width = queries.shape[1]
    if capacity != TILE * n or slots * width != 2 * TILE * kv_width:
        return per_device_small_pieces(
            cache_keys, cache_values, lengths, unfinished, send_slot, send_to, receive_from, land_slot, land_length,
            queries, new_keys, new_values, norm_gain, gate_weight, up_weight, down_weight
        )
    bf16, f32, i32 = jnp.bfloat16, jnp.float32, jnp.int32
    dma = pltpu.SemaphoreType.DMA
    pieces = (slots, n, TILE, kv_width)
    room = pltpu.CompilerParams(vmem_limit_bytes=16 * 2**20)
    hbm = spec(pltpu.HBM)

    def shape(dims, kind=bf16):
        return jax.ShapeDtypeStruct(dims, kind)

    def by_head(x):
        return x.reshape(slots, -1, HD).transpose(1, 0, 2)

    q, nk, nv = by_head(queries), by_head(new_keys), by_head(new_values)
    gain = norm_gain.reshape(HQ, HD)
    tokens = [VMEM(q.shape, bf16), VMEM(nk.shape, bf16), VMEM(nv.shape, bf16)]
    leaving = pl.pallas_call(
        pack_kernel,
        out_shape=shape((n, 2 * TILE, kv_width)),
        in_specs=[hbm] * 9,
        out_specs=spec(VMEM),
        scratch_shapes=[SMEM((n,), i32)] * 4 + tokens + [VMEM((TILE, kv_width), f32), dma((9,))],
        compiler_params=pltpu.CompilerParams(vmem_limit_bytes=60 * 2**20),
        cost_estimate=cost(0, 2**20),
        name="pack",
    )(
        send_slot, send_to, receive_from, land_slot, q, nk, nv, cache_keys.reshape(pieces), cache_values.reshape(pieces)
    )
    spread = exchange(leaving, GROUP)
    att, keys_own, values_own, given_row, pick = pl.pallas_call(
        local_kernel,
        out_shape=(
            shape((HQ, slots, HD), f32),
            shape(cache_keys.shape),
            shape(cache_keys.shape),
            shape((2, capacity, kv_width)),
            shape((n * slots, n * slots)),
        ),
        in_specs=[hbm] * 12,
        out_specs=(spec(VMEM), hbm, hbm, spec(VMEM), spec(VMEM)),
        scratch_shapes=[SMEM((n,), i32)] * 4 + [SMEM((slots,), i32)] * 2 + tokens + [
            VMEM((HQ, HD), f32),
            VMEM((HQ, slots, HD), f32),
            VMEM(cache_keys.shape, bf16),
            VMEM(cache_keys.shape, bf16),
            dma((2, slots)),
            dma((10,)),
            dma((2,)),
        ],
        compiler_params=room,
        cost_estimate=cost(2**24, 2**24),
        name="local",
    )(
        send_slot, send_to, receive_from, land_slot, lengths, unfinished, q, nk, nv, gain, cache_keys, cache_values
    )
    rows = pl.pallas_call(
        moved_kernel,
        out_shape=shape((chips, slots, width)),
        in_specs=[spec(SMEM)] * 3 + [spec(VMEM)] * 3 + [spec(pl.ANY)],
        out_specs=spec(VMEM),
        scratch_shapes=[
            VMEM((HQ, slots, HD), f32),
            VMEM((2, capacity, kv_width), bf16),
            VMEM((TILE, kv_width), bf16),
            dma,
        ],
        compiler_params=room,
        cost_estimate=cost(2**22, 2**20),
        name="moved",
    )(send_slot, send_to, lengths, gain, att, given_row, spread)
    near = exchange(rows, "chip")
    far = lax.ppermute(near, "core", [(0, 1), (1, 0)])
    outgoing = pl.pallas_call(
        select_kernel,
        out_shape=shape((n, 3 * TILE, kv_width)),
        in_specs=[spec(SMEM)] + [spec(pl.ANY)] * 2,
        out_specs=spec(pl.ANY),
        scratch_shapes=[dma((n,))],
        compiler_params=room,
        cost_estimate=cost(0, 2**20),
        name="select",
    )(receive_from, spread, near)
    mine, theirs = pl.pallas_call(
        ffn_kernel,
        out_shape=(shape((n * slots, width // 2), f32), shape((n * slots, width // 2))),
        in_specs=[spec(VMEM)] * 3 + [hbm] * 3,
        out_specs=(spec(VMEM), spec(VMEM)),
        scratch_shapes=[
            VMEM(gate_weight.shape, bf16),
            VMEM(up_weight.shape, bf16),
            VMEM(down_weight.shape, bf16),
            dma((3, CHUNKS)),
        ],
        compiler_params=pltpu.CompilerParams(vmem_limit_bytes=50 * 2**20),
        cost_estimate=cost(6 * n * slots * width * gate_weight.shape[1], 3 * 2**21),
        name="ffn",
    )(
        near.reshape(chips * slots, width), far.reshape(chips * slots, width), pick, gate_weight, up_weight, down_weight
    )
    theirs = lax.ppermute(theirs, "core", [(0, 1), (1, 0)])
    outgoing = pl.pallas_call(
        place_kernel,
        out_shape=shape((n, 3 * TILE, kv_width)),
        in_specs=[spec(VMEM)] * 2 + [spec(pl.ANY)],
        out_specs=spec(pl.ANY),
        scratch_shapes=[VMEM((n, TILE, kv_width), bf16), dma],
        input_output_aliases={2: 0},
        compiler_params=room,
        cost_estimate=cost(0, 2**20),
        name="place",
    )(mine, theirs, outgoing)
    arrived = exchange(outgoing, GROUP)
    decoded, keys_after, values_after = pl.pallas_call(
        finish_kernel,
        out_shape=(shape((slots, width)), shape(pieces), shape(pieces)),
        in_specs=[spec(SMEM)] * 3 + [spec(VMEM)] * 2 + [spec(pl.ANY)] * 3,
        out_specs=(spec(VMEM), spec(pl.ANY), spec(pl.ANY)),
        scratch_shapes=[
            VMEM((1, n, TILE, kv_width), bf16),
            VMEM((1, n, TILE, kv_width), bf16),
            VMEM((n, TILE, kv_width), bf16),
            dma((3,)),
        ],
        input_output_aliases={6: 1, 7: 2},
        compiler_params=room,
        cost_estimate=cost(0, 2**20),
        name="finish",
    )(
        receive_from, land_slot, land_length, nk, nv, arrived, keys_own.reshape(pieces), values_own.reshape(pieces)
    )
    return (decoded, keys_after.reshape(cache_keys.shape), values_after.reshape(cache_keys.shape))


def per_device_small_pieces(
    cache_keys,
    cache_values,
    lengths,
    unfinished,
    send_slot,
    send_to,
    receive_from,
    land_slot,
    land_length,
    queries,
    new_keys,
    new_values,
    norm_gain,
    gate_weight,
    up_weight,
    down_weight,
):
    group = GROUP
    me = lax.axis_index(group)
    chips, n = lax.axis_size("chip"), lax.axis_size(group)
    my_chip, my_core = lax.axis_index("chip"), lax.axis_index("core")
    slots, capacity, kv_width = cache_keys.shape
    width = queries.shape[1]
    slot_ids = jnp.arange(slots)
    target, source = send_to[me], receive_from[me]
    given_slot, taken_slot = send_slot[me], land_slot[me]
    giving, arriving = target != me, source != me
    landing = (slot_ids == taken_slot) & arriving
    vacated = (slot_ids == given_slot) & giving

    packet = jnp.concatenate(
        [
            lax.dynamic_index_in_dim(queries, taken_slot, 0, keepdims=False),
            lax.dynamic_index_in_dim(new_keys, taken_slot, 0, keepdims=False),
            lax.dynamic_index_in_dim(new_values, taken_slot, 0, keepdims=False),
        ]
    ).reshape(-1, 128)
    packets = exchange(jnp.broadcast_to(packet[None], (n,) + packet.shape), group)
    got = lax.dynamic_index_in_dim(packets, target, 0, keepdims=False).reshape(-1)

    rows = capacity // n
    leaving = jnp.concatenate(
        [
            lax.dynamic_index_in_dim(cache_keys, given_slot, 0, keepdims=False).reshape(n, rows, kv_width),
            lax.dynamic_index_in_dim(cache_values, given_slot, 0, keepdims=False).reshape(n, rows, kv_width),
        ],
        axis=1,
    )
    spread = exchange(leaving, group)

    row_queries = jnp.where(vacated[:, None], got[None, :width], queries)
    row_keys = jnp.where(vacated[:, None], got[None, width : width + kv_width], new_keys)
    row_values = jnp.where(vacated[:, None], got[None, width + kv_width :], new_values)
    row_alive = jnp.where(vacated, 1, jnp.where(landing, 0, unfinished)) > 0
    positions = jnp.arange(capacity)
    append = (positions[None, :] == lengths[:, None]) & row_alive[:, None]
    keys_here = jnp.where(append[:, :, None], row_keys[:, None, :], cache_keys)
    values_here = jnp.where(append[:, :, None], row_values[:, None, :], cache_values)
    query_heads = row_queries.reshape(slots, KVH, HQ // KVH, HD)
    key_heads = keys_here.reshape(slots, capacity, KVH, HD)
    value_heads = values_here.reshape(slots, capacity, KVH, HD)
    scores = jnp.einsum(
        "skgd,sckd->skgc", query_heads, key_heads, preferred_element_type=jnp.float32
    ) * (1.0 / math.sqrt(HD))
    visible = (positions[None, :] <= lengths[:, None])[:, None, None, :]
    scores = jnp.where(visible, scores, jnp.float32(-1e30))
    top = jnp.max(scores, axis=-1, keepdims=True)
    expo = jnp.exp(scores - top)
    probs = (expo / jnp.sum(expo, axis=-1, keepdims=True)).astype(jnp.bfloat16)
    attended = jnp.einsum(
        "skgc,sckd->skgd", probs, value_heads, preferred_element_type=jnp.float32
    ).reshape(slots, HQ * HD)
    mean_square = jnp.mean(attended * attended, axis=-1, keepdims=True)
    normed = attended * lax.rsqrt(mean_square + 1e-06) * norm_gain[None, :]
    normed = jnp.where(row_alive[:, None], normed, 0.0).astype(jnp.bfloat16)

    by_chip = exchange(jnp.broadcast_to(normed[None], (chips,) + normed.shape), "chip")
    other = lax.ppermute(by_chip, "core", [(0, 1), (1, 0)])

    chosen = jnp.take(spread, jnp.clip(receive_from, 0, n - 1), axis=0)
    arrived = exchange(chosen, group)
    arrived_keys = arrived[:, :rows].reshape(capacity, kv_width)
    arrived_values = arrived[:, rows:].reshape(capacity, kv_width)
    length_now = jnp.where(landing, land_length[me], lengths)
    alive = jnp.where(vacated, 0, jnp.where(landing, 1, unfinished)) > 0
    append_now = (positions[None, :] == length_now[:, None]) & alive[:, None]
    keys_after = jnp.where(landing[:, None, None], arrived_keys[None], cache_keys)
    values_after = jnp.where(landing[:, None, None], arrived_values[None], cache_values)
    keys_after = jnp.where(append_now[:, :, None], new_keys[:, None, :], keys_after)
    values_after = jnp.where(append_now[:, :, None], new_values[:, None, :], values_after)

    gathered = jnp.concatenate([by_chip, other], axis=0).reshape(n * slots, width)
    gate = jnp.dot(gathered, gate_weight, preferred_element_type=jnp.float32)
    up_part = jnp.dot(gathered, up_weight, preferred_element_type=jnp.float32)
    hidden = (jax.nn.silu(gate) * up_part).astype(jnp.bfloat16)
    everyone = jnp.arange(n)
    arrives = receive_from != everyone
    gives = send_to != everyone
    row_of = everyone[:, None] * slots + slot_ids[None, :]
    from_row = jnp.where(
        arrives[:, None] & (slot_ids[None, :] == land_slot[:, None]),
        (receive_from * slots + jnp.take(send_slot, jnp.clip(receive_from, 0, n - 1)))[:, None],
        row_of,
    )
    from_row = jnp.where(gives[:, None] & (slot_ids[None, :] == send_slot[:, None]), -1, from_row)
    order = jnp.concatenate([jnp.arange(chips) * 2 + 1 - my_core, jnp.arange(chips) * 2 + my_core])
    held = jnp.concatenate([jnp.arange(chips) * 2 + my_core, jnp.arange(chips) * 2 + 1 - my_core])
    wanted = jnp.take(from_row, order, axis=0).reshape(-1)
    held_row = (held[:, None] * slots + slot_ids[None, :]).reshape(-1)
    pick = (wanted[:, None] == held_row[None, :]).astype(jnp.bfloat16)
    placed_hidden = jnp.dot(pick, hidden, preferred_element_type=jnp.float32).astype(jnp.bfloat16)
    partial = jnp.dot(placed_hidden, down_weight, preferred_element_type=jnp.float32)
    half = chips * slots
    from_other = lax.ppermute(partial[:half].astype(jnp.bfloat16), "core", [(0, 1), (1, 0)])
    chip_sum = (partial[half:] + from_other.astype(jnp.float32)).astype(jnp.bfloat16)
    pieces = exchange(chip_sum.reshape(chips, slots, width), "chip")
    decoded = jnp.sum(pieces.astype(jnp.float32), axis=0).astype(jnp.bfloat16)
    return (decoded, keys_after, values_after)


def solution(mesh):
    parts, n = mesh.shape["parts"], mesh.shape["dp"]
    split = jax.sharding.Mesh(mesh.devices.reshape(parts, n // 2, 2), ("parts", "chip", "core"))
    every, own = ("parts", "chip", "core"), ("chip", "core")
    placed = (
        P(every, None, None),
        P(every, None, None),
        P(every),
        P(every),
        P("parts"),
        P("parts"),
        P("parts"),
        P("parts"),
        P("parts"),
        P(every, None),
        P(every, None),
        P(every, None),
        P(),
        P(None, own),
        P(None, own),
        P(own, None),
    )
    return jax.shard_map(
        per_device,
        mesh=split,
        in_specs=placed,
        out_specs=(P(every, None), P(every, None, None), P(every, None, None)),
        check_vma=False,
    )
```

```python
import math

import jax
import jax.numpy as jnp
from jax import lax
from jax.experimental import pallas as pl
from jax.experimental.pallas import tpu as pltpu
from jax.sharding import PartitionSpec as P

HQ = 32
KVH = 4
HD = 128
PER = HQ // KVH
TILE = 16
CHUNKS = 4
GROUP = ("chip", "core")
SMEM, VMEM = pltpu.SMEM, pltpu.VMEM


def exchange(blocks, axis):
    return lax.all_to_all(blocks, axis, 0, 0, tiled=True)


def spec(space):
    return pl.BlockSpec(memory_space=space)


def cost(flops, moved):
    return pl.CostEstimate(flops=flops, bytes_accessed=moved, transcendentals=0)


def pack_kernel(
    send_slot, send_to, receive_from, land_slot, q, nk, nv, ck, cv, leaving,
    slot_s, to_s, from_s, land_s, qb, kb, vb, whole, packet, tile, sems
):
    me = lax.axis_index(GROUP)
    slots = q.shape[1]
    fetches = [
        pltpu.make_async_copy(a, b, sems.at[2 + i])
        for i, (a, b) in enumerate(
            (
                (send_slot, slot_s), (send_to, to_s), (receive_from, from_s), (land_slot, land_s),
                (q, qb), (nk, kb), (nv, vb),
            )
        )
    ]
    for fetch in fetches:
        fetch.start()
    for fetch in fetches[:4]:
        fetch.wait()
    giving = to_s[me] != me
    copies = [pltpu.make_async_copy(cache.at[slot_s[me]], whole.at[i], sems.at[i]) for i, cache in enumerate((ck, cv))]
    stores = [
        pltpu.make_async_copy(whole.at[i], leaving.at[:, pl.ds(i * TILE, TILE)], sems.at[9 + i]) for i in range(2)
    ]

    @pl.when(giving)
    def _():
        for copy in copies:
            copy.start()

    for fetch in fetches[4:]:
        fetch.wait()

    @pl.when(giving)
    def _():
        for copy, store in zip(copies, stores):
            copy.wait()
            store.start()
        for store in stores:
            store.wait()

    @pl.when(jnp.logical_not(giving))
    def _():
        taken = land_s[me]

        def line(x):
            mine = lax.broadcasted_iota(jnp.int32, (x.shape[0], slots, HD), 1) == taken
            return jnp.sum(jnp.where(mine, x[...].astype(jnp.float32), 0.0), axis=1)

        heads, key, value = line(qb), line(kb), line(vb)
        packet[...] = jnp.zeros_like(packet)
        for k in range(KVH):
            columns = slice(k * HD, (k + 1) * HD)
            packet[0:PER, columns] = heads[k * PER : (k + 1) * PER]
            packet[PER : PER + 1, columns] = key[k : k + 1]
            packet[PER + 1 : PER + 2, columns] = value[k : k + 1]
        tile[...] = packet[...].astype(jnp.bfloat16)
        send = pltpu.make_async_copy(tile, leaving.at[from_s[me], pl.ds(0, TILE)], sems.at[0])
        send.start()
        send.wait()


def put_line(buf, at, base, line, fresh):
    here = lax.broadcasted_iota(jnp.int32, (TILE, HD), 0) == line
    for k in range(KVH):
        columns = slice(k * HD, (k + 1) * HD)
        old = buf[at, pl.ds(base, TILE), columns].astype(jnp.float32)
        buf[at, pl.ds(base, TILE), columns] = jnp.where(here, fresh[k], old).astype(jnp.bfloat16)


def place_of(length, alive):
    block = length // TILE
    return pl.multiple_of(block * TILE, TILE), jnp.where(alive, length - block * TILE, -1)


def attend(heads, kbuf, vbuf, at, length, gain):
    scores = jnp.concatenate(
        [
            lax.dot_general(
                heads[k].astype(jnp.bfloat16),
                kbuf[at, :, k * HD : (k + 1) * HD],
                (((1,), (1,)), ((), ())),
                preferred_element_type=jnp.float32,
            )
            for k in range(KVH)
        ],
        axis=0,
    )
    visible = lax.broadcasted_iota(jnp.int32, scores.shape, 1) <= length
    scores = jnp.where(visible, scores * (1.0 / math.sqrt(HD)), jnp.float32(-1e30))
    expo = jnp.exp(scores - jnp.max(scores, axis=1, keepdims=True))
    probs = expo / jnp.sum(expo, axis=1, keepdims=True)
    attended = jnp.concatenate(
        [
            jnp.dot(
                probs[k * PER : (k + 1) * PER].astype(jnp.bfloat16),
                vbuf[at, :, k * HD : (k + 1) * HD],
                preferred_element_type=jnp.float32,
            )
            for k in range(KVH)
        ],
        axis=0,
    )
    mean = jnp.sum(attended * attended, keepdims=True) * (1.0 / (HQ * HD))
    return attended * lax.rsqrt(mean + 1e-06) * gain


def local_kernel(
    send_slot, send_to, receive_from, land_slot, lengths, unfinished, q, nk, nv, gain, ck, cv,
    att, keys, values, given_row, pick,
    slot_s, to_s, from_s, land_s, length_s, left_s, qb, kb, vb, gb, q32, kbuf, vbuf, sems, small, big
):
    me = lax.axis_index(GROUP)
    core = lax.axis_index("core")
    slots, n, rows = ck.shape[0], slot_s.shape[0], pick.shape[0]
    half = rows // 2
    pairs = ((ck, kbuf, keys), (cv, vbuf, values))
    fetches = [
        pltpu.make_async_copy(a, b, small.at[i])
        for i, (a, b) in enumerate(
            (
                (send_slot, slot_s), (send_to, to_s), (receive_from, from_s), (land_slot, land_s),
                (lengths, length_s), (unfinished, left_s), (q, qb), (nk, kb), (nv, vb), (gain, gb),
            )
        )
    ]
    for fetch in fetches:
        fetch.start()

    def load(i, j):
        return pltpu.make_async_copy(pairs[i][0].at[j], pairs[i][1].at[j], sems.at[i, j])

    def store(i, j):
        return pltpu.make_async_copy(pairs[i][1].at[j], pairs[i][2].at[j], sems.at[i, j])

    for j in range(slots):
        for i in range(2):
            load(i, j).start()
    for fetch in fetches:
        fetch.wait()
    large = [pltpu.make_async_copy(pairs[i][0].at[slot_s[me]], given_row.at[i], big.at[i]) for i in range(2)]
    for copy in large:
        copy.start()
    row = lax.broadcasted_iota(jnp.int32, (rows, HD), 0)
    device = row // slots
    wanted = jnp.where((device & 1) == core, 0, half) + (device >> 1) * slots + (row & (slots - 1))
    for d in range(n):
        source = from_s[d]
        held = jnp.where(lax.rem(source, 2) == core, 0, half) + (source // 2) * slots + slot_s[source]
        landing = jnp.where(source != d, d * slots + land_s[d], -1)
        vacated = jnp.where(to_s[d] != d, d * slots + slot_s[d], -1)
        wanted = jnp.where(row == landing, held, wanted)
        wanted = jnp.where(row == vacated, -1, wanted)
    column = lax.broadcasted_iota(jnp.int32, (rows, rows), 1)
    pick[...] = (column == wanted[:, :1]).astype(jnp.float32).astype(jnp.bfloat16)
    q32[...] = qb[...].astype(jnp.float32)
    for j in range(slots):
        vacated = (to_s[me] != me) & (slot_s[me] == j)
        alive = jnp.where(vacated, 0, left_s[j]) > 0
        length = length_s[j]
        base, line = place_of(length, alive)
        for i, own in enumerate((kb, vb)):
            load(i, j).wait()
            put_line(pairs[i][1], j, base, line, [own[k, j : j + 1].astype(jnp.float32) for k in range(KVH)])
            store(i, j).start()
        own_heads = q32[:, j, :]
        normed = attend([own_heads[k * PER : (k + 1) * PER] for k in range(KVH)], kbuf, vbuf, j, length, gb[...])
        att[:, j, :] = jnp.where(alive, normed, 0.0)
    for j in range(slots):
        for i in range(2):
            store(i, j).wait()
    for copy in large:
        copy.wait()


def moved_kernel(send_slot, send_to, lengths, gain, att, given_row, spread, out, mine, kv):
    me = lax.axis_index(GROUP)
    mine[...] = att[...]

    @pl.when(send_to[me] != me)
    def _():
        kv[...] = given_row[...]
        slots = mine.shape[1]
        given = send_slot[me]
        length = lengths[given]
        base, line = place_of(length, True)
        packet = spread[send_to[me], 0:TILE].astype(jnp.float32)
        for i in range(2):
            put_line(kv, i, base, line, [packet[PER + i : PER + i + 1, k * HD : (k + 1) * HD] for k in range(KVH)])
        heads = [packet[0:PER, k * HD : (k + 1) * HD] for k in range(KVH)]
        normed = attend(heads, kv.at[0:1], kv.at[1:2], 0, length, gain[...])
        for j in range(slots):
            pl.when(given == j)(lambda j=j: mine.__setitem__((slice(None), j, slice(None)), normed))

    for h in range(HQ):
        head = mine[h].astype(jnp.bfloat16)
        for c in range(out.shape[0]):
            out[c, :, h * HD : (h + 1) * HD] = head


def select_kernel(receive_from, spread, _, outgoing, piece_sem):
    n = outgoing.shape[0]

    def piece(d):
        return pltpu.make_async_copy(spread.at[receive_from[d]], outgoing.at[d, pl.ds(0, 2 * TILE)], piece_sem.at[d])

    for d in range(n):
        pl.when(receive_from[d] != d)(lambda d=d: piece(d).start())
    for d in range(n):
        pl.when(receive_from[d] != d)(lambda d=d: piece(d).wait())


def ffn_kernel(near, far, pick, gate_weight, up_weight, down_weight, mine, theirs, up_v, down_v, sems):
    core = lax.axis_index("core")
    width = mine.shape[1]
    step = up_v.shape[0] // CHUNKS
    sides = [pl.ds(pl.multiple_of(side * width, width), width) for side in (1 - core, core)]
    chunks = [pl.ds(c * step, step) for c in range(CHUNKS)]
    ups = [pltpu.make_async_copy(up_weight.at[at], up_v.at[at], sems.at[0, c]) for c, at in enumerate(chunks)]
    downs = [pltpu.make_async_copy(down_weight.at[:, at], down_v.at[:, at], sems.at[1, i]) for i, at in enumerate(sides)]
    for load in ups + downs:
        load.start()
    x = jnp.concatenate([near[...], far[...]], axis=0)
    gate = jnp.dot(x, gate_weight[...], preferred_element_type=jnp.float32)
    up_part = 0.0
    for c in range(CHUNKS):
        at = slice(c * step, (c + 1) * step)
        x = jnp.concatenate([near[:, at], far[:, at]], axis=0)
        ups[c].wait()
        up_part += jnp.dot(x, up_v[at], preferred_element_type=jnp.float32)
    hidden = (gate / (1.0 + jnp.exp(-gate)) * up_part).astype(jnp.bfloat16)
    hidden = jnp.dot(pick[...], hidden, preferred_element_type=jnp.float32).astype(jnp.bfloat16)
    downs[0].wait()
    theirs[...] = jnp.dot(hidden, down_v[:, sides[0]], preferred_element_type=jnp.float32).astype(jnp.bfloat16)
    downs[1].wait()
    mine[...] = jnp.dot(hidden, down_v[:, sides[1]], preferred_element_type=jnp.float32)


def place_kernel(mine, theirs, outgoing, out, rows, sem):
    n, _, wide = rows.shape
    slots = mine.shape[0] // n
    for d in range(n):
        at = slice(d * slots, (d + 1) * slots)
        both = mine[at] + theirs[at].astype(jnp.float32)
        rows[d] = jnp.concatenate(
            [both[:, g * wide : (g + 1) * wide] for g in range(both.shape[1] // wide)], axis=0
        ).astype(jnp.bfloat16)
    copy = pltpu.make_async_copy(rows, out.at[:, pl.ds(2 * TILE, TILE)], sem)
    copy.start()
    copy.wait()


def finish_kernel(
    receive_from, land_slot, land_length, nk, nv, arrived, keys_in, values_in, decoded, keys, values, whole, sems
):
    me = lax.axis_index(GROUP)
    n, wide = arrived.shape[0], arrived.shape[2]
    slots, slot = decoded.shape[0], land_slot[me]
    arriving = receive_from[me] != me
    length = land_length[me]
    block = length // TILE
    outs = ((keys, nk), (values, nv))
    stores = [pltpu.make_async_copy(whole.at[i], outs[i][0].at[slot], sems.at[i]) for i in range(2)]

    @pl.when(arriving)
    def _():
        here = lax.broadcasted_iota(jnp.int32, (TILE, HD), 0) == length - block * TILE
        for i in range(2):
            own = outs[i][1]
            mine = lax.broadcasted_iota(jnp.int32, (KVH, slots, HD), 1) == slot
            token = jnp.sum(jnp.where(mine, own[...].astype(jnp.float32), 0.0), axis=1)
            for d in range(n):
                whole[i, d] = arrived[d, i * TILE : (i + 1) * TILE]
            for k in range(KVH):
                columns = slice(k * HD, (k + 1) * HD)
                old = arrived[block, i * TILE : (i + 1) * TILE, columns].astype(jnp.float32)
                whole[i, block, :, columns] = jnp.where(here, token[k : k + 1], old).astype(jnp.bfloat16)
            stores[i].start()

    for side in range(2):
        total = arrived[side, 2 * TILE : 3 * TILE].astype(jnp.float32)
        for c in range(1, n // 2):
            total += arrived[2 * c + side, 2 * TILE : 3 * TILE].astype(jnp.float32)
        for g in range(TILE // slots):
            at = (side * (TILE // slots) + g) * wide
            decoded[:, at : at + wide] = total[g * slots : (g + 1) * slots].astype(jnp.bfloat16)

    @pl.when(arriving)
    def _():
        for store in stores:
            store.wait()


def per_device(
    cache_keys, cache_values, lengths, unfinished, send_slot, send_to, receive_from, land_slot, land_length,
    queries, new_keys, new_values, norm_gain, gate_weight, up_weight, down_weight
):
    chips, n = lax.axis_size("chip"), lax.axis_size(GROUP)
    slots, capacity, kv_width = cache_keys.shape
    width = queries.shape[1]
    if capacity != TILE * n or slots * width != 2 * TILE * kv_width:
        return per_device_small_pieces(
            cache_keys, cache_values, lengths, unfinished, send_slot, send_to, receive_from, land_slot, land_length,
            queries, new_keys, new_values, norm_gain, gate_weight, up_weight, down_weight
        )
    bf16, f32, i32 = jnp.bfloat16, jnp.float32, jnp.int32
    dma = pltpu.SemaphoreType.DMA
    pieces = (slots, n, TILE, kv_width)
    room = pltpu.CompilerParams(vmem_limit_bytes=16 * 2**20)
    hbm = spec(pltpu.HBM)

    def shape(dims, kind=bf16):
        return jax.ShapeDtypeStruct(dims, kind)

    def by_head(x):
        return x.reshape(slots, -1, HD).transpose(1, 0, 2)

    q, nk, nv = by_head(queries), by_head(new_keys), by_head(new_values)
    gain = norm_gain.reshape(HQ, HD)
    tokens = [VMEM(q.shape, bf16), VMEM(nk.shape, bf16), VMEM(nv.shape, bf16)]
    leaving = pl.pallas_call(
        pack_kernel,
        out_shape=shape((n, 2 * TILE, kv_width)),
        in_specs=[hbm] * 9,
        out_specs=hbm,
        scratch_shapes=[SMEM((n,), i32)] * 4 + tokens + [
            VMEM((2, n, TILE, kv_width), bf16), VMEM((TILE, kv_width), f32), VMEM((TILE, kv_width), bf16), dma((11,))
        ],
        compiler_params=pltpu.CompilerParams(vmem_limit_bytes=60 * 2**20),
        cost_estimate=cost(0, 2**20),
        name="pack",
    )(
        send_slot, send_to, receive_from, land_slot, q, nk, nv, cache_keys.reshape(pieces), cache_values.reshape(pieces)
    )
    spread = exchange(leaving, GROUP)
    att, keys_own, values_own, given_row, pick = pl.pallas_call(
        local_kernel,
        out_shape=(
            shape((HQ, slots, HD), f32),
            shape(cache_keys.shape),
            shape(cache_keys.shape),
            shape((2, capacity, kv_width)),
            shape((n * slots, n * slots)),
        ),
        in_specs=[hbm] * 12,
        out_specs=(spec(VMEM), hbm, hbm, spec(VMEM), spec(VMEM)),
        scratch_shapes=[SMEM((n,), i32)] * 4 + [SMEM((slots,), i32)] * 2 + tokens + [
            VMEM((HQ, HD), f32),
            VMEM((HQ, slots, HD), f32),
            VMEM(cache_keys.shape, bf16),
            VMEM(cache_keys.shape, bf16),
            dma((2, slots)),
            dma((10,)),
            dma((2,)),
        ],
        compiler_params=room,
        cost_estimate=cost(2**24, 2**24),
        name="local",
    )(
        send_slot, send_to, receive_from, land_slot, lengths, unfinished, q, nk, nv, gain, cache_keys, cache_values
    )
    rows = pl.pallas_call(
        moved_kernel,
        out_shape=shape((chips, slots, width)),
        in_specs=[spec(SMEM)] * 3 + [spec(VMEM)] * 4,
        out_specs=spec(VMEM),
        scratch_shapes=[VMEM((HQ, slots, HD), f32), VMEM((2, capacity, kv_width), bf16)],
        compiler_params=room,
        cost_estimate=cost(2**22, 2**20),
        name="moved",
    )(send_slot, send_to, lengths, gain, att, given_row, spread)
    near = exchange(rows, "chip")
    near = near.reshape(chips * slots, width)
    far = lax.ppermute(near, "core", [(0, 1), (1, 0)])
    outgoing = pl.pallas_call(
        select_kernel,
        out_shape=shape((n, 3 * TILE, kv_width)),
        in_specs=[spec(SMEM)] + [spec(pl.ANY)] * 2,
        out_specs=spec(pl.ANY),
        scratch_shapes=[dma((n,))],
        compiler_params=room,
        cost_estimate=cost(0, 2**20),
        name="select",
    )(receive_from, spread, near)
    far, outgoing = lax.optimization_barrier((far, outgoing))
    mine, theirs = pl.pallas_call(
        ffn_kernel,
        out_shape=(shape((n * slots, width // 2), f32), shape((n * slots, width // 2))),
        in_specs=[spec(VMEM)] * 4 + [hbm] * 2,
        out_specs=(spec(VMEM), spec(VMEM)),
        scratch_shapes=[
            VMEM(up_weight.shape, bf16),
            VMEM(down_weight.shape, bf16),
            dma((2, CHUNKS)),
        ],
        compiler_params=pltpu.CompilerParams(vmem_limit_bytes=50 * 2**20),
        cost_estimate=cost(6 * n * slots * width * gate_weight.shape[1], 3 * 2**21),
        name="ffn",
    )(
        near, far, pick, gate_weight, up_weight, down_weight
    )
    theirs = lax.ppermute(theirs, "core", [(0, 1), (1, 0)])
    outgoing = pl.pallas_call(
        place_kernel,
        out_shape=shape((n, 3 * TILE, kv_width)),
        in_specs=[spec(VMEM)] * 2 + [spec(pl.ANY)],
        out_specs=spec(pl.ANY),
        scratch_shapes=[VMEM((n, TILE, kv_width), bf16), dma],
        input_output_aliases={2: 0},
        compiler_params=room,
        cost_estimate=cost(0, 2**20),
        name="place",
    )(mine, theirs, outgoing)
    arrived = exchange(outgoing, GROUP)
    decoded, keys_after, values_after = pl.pallas_call(
        finish_kernel,
        out_shape=(shape((slots, width)), shape(pieces), shape(pieces)),
        in_specs=[spec(SMEM)] * 3 + [spec(VMEM)] * 3 + [spec(pl.ANY)] * 2,
        out_specs=(spec(VMEM), spec(pl.ANY), spec(pl.ANY)),
        scratch_shapes=[VMEM((2, n, TILE, kv_width), bf16), dma((2,))],
        input_output_aliases={6: 1, 7: 2},
        compiler_params=room,
        cost_estimate=cost(0, 2**20),
        name="finish",
    )(
        receive_from, land_slot, land_length, nk, nv, arrived, keys_own.reshape(pieces), values_own.reshape(pieces)
    )
    return (decoded, keys_after.reshape(cache_keys.shape), values_after.reshape(cache_keys.shape))


def per_device_small_pieces(
    cache_keys,
    cache_values,
    lengths,
    unfinished,
    send_slot,
    send_to,
    receive_from,
    land_slot,
    land_length,
    queries,
    new_keys,
    new_values,
    norm_gain,
    gate_weight,
    up_weight,
    down_weight,
):
    group = GROUP
    me = lax.axis_index(group)
    chips, n = lax.axis_size("chip"), lax.axis_size(group)
    my_chip, my_core = lax.axis_index("chip"), lax.axis_index("core")
    slots, capacity, kv_width = cache_keys.shape
    width = queries.shape[1]
    slot_ids = jnp.arange(slots)
    target, source = send_to[me], receive_from[me]
    given_slot, taken_slot = send_slot[me], land_slot[me]
    giving, arriving = target != me, source != me
    landing = (slot_ids == taken_slot) & arriving
    vacated = (slot_ids == given_slot) & giving

    packet = jnp.concatenate(
        [
            lax.dynamic_index_in_dim(queries, taken_slot, 0, keepdims=False),
            lax.dynamic_index_in_dim(new_keys, taken_slot, 0, keepdims=False),
            lax.dynamic_index_in_dim(new_values, taken_slot, 0, keepdims=False),
        ]
    ).reshape(-1, 128)
    packets = exchange(jnp.broadcast_to(packet[None], (n,) + packet.shape), group)
    got = lax.dynamic_index_in_dim(packets, target, 0, keepdims=False).reshape(-1)

    rows = capacity // n
    leaving = jnp.concatenate(
        [
            lax.dynamic_index_in_dim(cache_keys, given_slot, 0, keepdims=False).reshape(n, rows, kv_width),
            lax.dynamic_index_in_dim(cache_values, given_slot, 0, keepdims=False).reshape(n, rows, kv_width),
        ],
        axis=1,
    )
    spread = exchange(leaving, group)

    row_queries = jnp.where(vacated[:, None], got[None, :width], queries)
    row_keys = jnp.where(vacated[:, None], got[None, width : width + kv_width], new_keys)
    row_values = jnp.where(vacated[:, None], got[None, width + kv_width :], new_values)
    row_alive = jnp.where(vacated, 1, jnp.where(landing, 0, unfinished)) > 0
    positions = jnp.arange(capacity)
    append = (positions[None, :] == lengths[:, None]) & row_alive[:, None]
    keys_here = jnp.where(append[:, :, None], row_keys[:, None, :], cache_keys)
    values_here = jnp.where(append[:, :, None], row_values[:, None, :], cache_values)
    query_heads = row_queries.reshape(slots, KVH, HQ // KVH, HD)
    key_heads = keys_here.reshape(slots, capacity, KVH, HD)
    value_heads = values_here.reshape(slots, capacity, KVH, HD)
    scores = jnp.einsum(
        "skgd,sckd->skgc", query_heads, key_heads, preferred_element_type=jnp.float32
    ) * (1.0 / math.sqrt(HD))
    visible = (positions[None, :] <= lengths[:, None])[:, None, None, :]
    scores = jnp.where(visible, scores, jnp.float32(-1e30))
    top = jnp.max(scores, axis=-1, keepdims=True)
    expo = jnp.exp(scores - top)
    probs = (expo / jnp.sum(expo, axis=-1, keepdims=True)).astype(jnp.bfloat16)
    attended = jnp.einsum(
        "skgc,sckd->skgd", probs, value_heads, preferred_element_type=jnp.float32
    ).reshape(slots, HQ * HD)
    mean_square = jnp.mean(attended * attended, axis=-1, keepdims=True)
    normed = attended * lax.rsqrt(mean_square + 1e-06) * norm_gain[None, :]
    normed = jnp.where(row_alive[:, None], normed, 0.0).astype(jnp.bfloat16)

    by_chip = exchange(jnp.broadcast_to(normed[None], (chips,) + normed.shape), "chip")
    other = lax.ppermute(by_chip, "core", [(0, 1), (1, 0)])

    chosen = jnp.take(spread, jnp.clip(receive_from, 0, n - 1), axis=0)
    arrived = exchange(chosen, group)
    arrived_keys = arrived[:, :rows].reshape(capacity, kv_width)
    arrived_values = arrived[:, rows:].reshape(capacity, kv_width)
    length_now = jnp.where(landing, land_length[me], lengths)
    alive = jnp.where(vacated, 0, jnp.where(landing, 1, unfinished)) > 0
    append_now = (positions[None, :] == length_now[:, None]) & alive[:, None]
    keys_after = jnp.where(landing[:, None, None], arrived_keys[None], cache_keys)
    values_after = jnp.where(landing[:, None, None], arrived_values[None], cache_values)
    keys_after = jnp.where(append_now[:, :, None], new_keys[:, None, :], keys_after)
    values_after = jnp.where(append_now[:, :, None], new_values[:, None, :], values_after)

    gathered = jnp.concatenate([by_chip, other], axis=0).reshape(n * slots, width)
    gate = jnp.dot(gathered, gate_weight, preferred_element_type=jnp.float32)
    up_part = jnp.dot(gathered, up_weight, preferred_element_type=jnp.float32)
    hidden = (jax.nn.silu(gate) * up_part).astype(jnp.bfloat16)
    everyone = jnp.arange(n)
    arrives = receive_from != everyone
    gives = send_to != everyone
    row_of = everyone[:, None] * slots + slot_ids[None, :]
    from_row = jnp.where(
        arrives[:, None] & (slot_ids[None, :] == land_slot[:, None]),
        (receive_from * slots + jnp.take(send_slot, jnp.clip(receive_from, 0, n - 1)))[:, None],
        row_of,
    )
    from_row = jnp.where(gives[:, None] & (slot_ids[None, :] == send_slot[:, None]), -1, from_row)
    order = jnp.concatenate([jnp.arange(chips) * 2 + 1 - my_core, jnp.arange(chips) * 2 + my_core])
    held = jnp.concatenate([jnp.arange(chips) * 2 + my_core, jnp.arange(chips) * 2 + 1 - my_core])
    wanted = jnp.take(from_row, order, axis=0).reshape(-1)
    held_row = (held[:, None] * slots + slot_ids[None, :]).reshape(-1)
    pick = (wanted[:, None] == held_row[None, :]).astype(jnp.bfloat16)
    placed_hidden = jnp.dot(pick, hidden, preferred_element_type=jnp.float32).astype(jnp.bfloat16)
    partial = jnp.dot(placed_hidden, down_weight, preferred_element_type=jnp.float32)
    half = chips * slots
    from_other = lax.ppermute(partial[:half].astype(jnp.bfloat16), "core", [(0, 1), (1, 0)])
    chip_sum = (partial[half:] + from_other.astype(jnp.float32)).astype(jnp.bfloat16)
    pieces = exchange(chip_sum.reshape(chips, slots, width), "chip")
    decoded = jnp.sum(pieces.astype(jnp.float32), axis=0).astype(jnp.bfloat16)
    return (decoded, keys_after, values_after)


def solution(mesh):
    parts, n = mesh.shape["parts"], mesh.shape["dp"]
    split = jax.sharding.Mesh(mesh.devices.reshape(parts, n // 2, 2), ("parts", "chip", "core"))
    every, own = ("parts", "chip", "core"), ("chip", "core")
    placed = (
        P(every, None, None),
        P(every, None, None),
        P(every),
        P(every),
        P("parts"),
        P("parts"),
        P("parts"),
        P("parts"),
        P("parts"),
        P(every, None),
        P(every, None),
        P(every, None),
        P(),
        P(None, own),
        P(None, own),
        P(own, None),
    )
    return jax.shard_map(
        per_device,
        mesh=split,
        in_specs=placed,
        out_specs=(P(every, None), P(every, None, None), P(every, None, None)),
        check_vma=False,
    )
```

```python
import math

import jax
import jax.numpy as jnp
from jax import lax
from jax.experimental import pallas as pl
from jax.experimental.pallas import tpu as pltpu
from jax.sharding import PartitionSpec as P

HQ = 32
KVH = 4
HD = 128
PER = HQ // KVH
TILE = 16
CHUNKS = 4
GROUP = ("chip", "core")
SMEM, VMEM = pltpu.SMEM, pltpu.VMEM


def exchange(blocks, axis):
    return lax.all_to_all(blocks, axis, 0, 0, tiled=True)


def spec(space):
    return pl.BlockSpec(memory_space=space)


def cost(flops, moved):
    return pl.CostEstimate(flops=flops, bytes_accessed=moved, transcendentals=0)


def pack_kernel(
    send_slot, send_to, receive_from, land_slot, q, nk, nv, ck, cv, leaving,
    slot_s, to_s, from_s, land_s, qb, kb, vb, whole, packet, tile, sems
):
    me = lax.axis_index(GROUP)
    slots = q.shape[1]
    fetches = [
        pltpu.make_async_copy(a, b, sems.at[2 + i])
        for i, (a, b) in enumerate(
            (
                (send_slot, slot_s), (send_to, to_s), (receive_from, from_s), (land_slot, land_s),
                (q, qb), (nk, kb), (nv, vb),
            )
        )
    ]
    for fetch in fetches:
        fetch.start()
    loads = [pltpu.make_async_copy(cache, whole.at[i], sems.at[i]) for i, cache in enumerate((ck, cv))]
    for load in loads:
        load.start()
    for fetch in fetches:
        fetch.wait()
    giving = to_s[me] != me
    stores = [
        pltpu.make_async_copy(whole.at[i, slot_s[me]], leaving.at[:, pl.ds(i * TILE, TILE)], sems.at[9 + i]) for i in range(2)
    ]

    for load, store in zip(loads, stores):
        load.wait()
        pl.when(giving)(store.start)

    @pl.when(giving)
    def _():
        for store in stores:
            store.wait()

    @pl.when(jnp.logical_not(giving))
    def _():
        taken = land_s[me]

        def line(x):
            mine = lax.broadcasted_iota(jnp.int32, (x.shape[0], slots, HD), 1) == taken
            return jnp.sum(jnp.where(mine, x[...].astype(jnp.float32), 0.0), axis=1)

        heads, key, value = line(qb), line(kb), line(vb)
        packet[...] = jnp.zeros_like(packet)
        for k in range(KVH):
            columns = slice(k * HD, (k + 1) * HD)
            packet[0:PER, columns] = heads[k * PER : (k + 1) * PER]
            packet[PER : PER + 1, columns] = key[k : k + 1]
            packet[PER + 1 : PER + 2, columns] = value[k : k + 1]
        tile[...] = packet[...].astype(jnp.bfloat16)
        send = pltpu.make_async_copy(tile, leaving.at[from_s[me], pl.ds(0, TILE)], sems.at[0])
        send.start()
        send.wait()


def put_line(buf, at, base, line, fresh):
    here = lax.broadcasted_iota(jnp.int32, (TILE, HD), 0) == line
    for k in range(KVH):
        columns = slice(k * HD, (k + 1) * HD)
        old = buf[at, pl.ds(base, TILE), columns].astype(jnp.float32)
        buf[at, pl.ds(base, TILE), columns] = jnp.where(here, fresh[k], old).astype(jnp.bfloat16)


def place_of(length, alive):
    block = length // TILE
    return pl.multiple_of(block * TILE, TILE), jnp.where(alive, length - block * TILE, -1)


def attend(heads, kbuf, vbuf, at, length, gain, token=None):
    scores = jnp.concatenate(
        [
            lax.dot_general(
                heads[k].astype(jnp.bfloat16),
                kbuf[at, :, k * HD : (k + 1) * HD],
                (((1,), (1,)), ((), ())),
                preferred_element_type=jnp.float32,
            )
            for k in range(KVH)
        ],
        axis=0,
    )
    position = lax.broadcasted_iota(jnp.int32, scores.shape, 1)
    if token is not None:
        fresh = [jnp.sum(heads[k] * token[0][k], axis=1, keepdims=True) for k in range(KVH)]
        scores = jnp.where(position == length, jnp.concatenate(fresh, axis=0), scores)
    scores = jnp.where(position <= length, scores * (1.0 / math.sqrt(HD)), jnp.float32(-1e30))
    expo = jnp.exp(scores - jnp.max(scores, axis=1, keepdims=True))
    probs = expo / jnp.sum(expo, axis=1, keepdims=True)
    if token is not None:
        last = jnp.sum(jnp.where(position == length, probs, 0.0), axis=1, keepdims=True)
        last = last.astype(jnp.bfloat16).astype(jnp.float32)
        probs = jnp.where(position == length, 0.0, probs)
    parts = [
        jnp.dot(
            probs[k * PER : (k + 1) * PER].astype(jnp.bfloat16),
            vbuf[at, :, k * HD : (k + 1) * HD],
            preferred_element_type=jnp.float32,
        )
        for k in range(KVH)
    ]
    if token is not None:
        parts = [parts[k] + last[k * PER : (k + 1) * PER] * token[1][k] for k in range(KVH)]
    attended = jnp.concatenate(parts, axis=0)
    mean = jnp.sum(attended * attended, keepdims=True) * (1.0 / (HQ * HD))
    return attended * lax.rsqrt(mean + 1e-06) * gain


def local_kernel(
    send_slot, send_to, receive_from, land_slot, lengths, unfinished, q, nk, nv, gain, ck, cv,
    att, keys, values, given_row, pick,
    slot_s, to_s, from_s, land_s, length_s, left_s, qb, kb, vb, gb, q32, kbuf, vbuf, sems, small, big
):
    me = lax.axis_index(GROUP)
    core = lax.axis_index("core")
    slots, n, rows = ck.shape[0], slot_s.shape[0], pick.shape[0]
    half = rows // 2
    pairs = ((ck, kbuf, keys), (cv, vbuf, values))
    fetches = [
        pltpu.make_async_copy(a, b, small.at[i])
        for i, (a, b) in enumerate(
            (
                (send_slot, slot_s), (send_to, to_s), (receive_from, from_s), (land_slot, land_s),
                (lengths, length_s), (unfinished, left_s), (q, qb), (nk, kb), (nv, vb), (gain, gb),
            )
        )
    ]
    for fetch in fetches:
        fetch.start()

    def load(i, j):
        return pltpu.make_async_copy(pairs[i][0].at[j], pairs[i][1].at[j], sems.at[i, j])

    def store(i, j):
        return pltpu.make_async_copy(pairs[i][1].at[j], pairs[i][2].at[j], sems.at[i, j])

    for j in range(slots):
        for i in range(2):
            load(i, j).start()
    for fetch in fetches:
        fetch.wait()
    large = [pltpu.make_async_copy(pairs[i][0].at[slot_s[me]], given_row.at[i], big.at[i]) for i in range(2)]
    for copy in large:
        copy.start()
    row = lax.broadcasted_iota(jnp.int32, (rows, HD), 0)
    device = row // slots
    wanted = jnp.where((device & 1) == core, 0, half) + (device >> 1) * slots + (row & (slots - 1))
    for d in range(n):
        source = from_s[d]
        held = jnp.where(lax.rem(source, 2) == core, 0, half) + (source // 2) * slots + slot_s[source]
        landing = jnp.where(source != d, d * slots + land_s[d], -1)
        vacated = jnp.where(to_s[d] != d, d * slots + slot_s[d], -1)
        wanted = jnp.where(row == landing, held, wanted)
        wanted = jnp.where(row == vacated, -1, wanted)
    column = lax.broadcasted_iota(jnp.int32, (rows, rows), 1)
    pick[...] = (column == wanted[:, :1]).astype(jnp.float32).astype(jnp.bfloat16)
    q32[...] = qb[...].astype(jnp.float32)
    for j in range(slots):
        vacated = (to_s[me] != me) & (slot_s[me] == j)
        alive = jnp.where(vacated, 0, left_s[j]) > 0
        length = length_s[j]
        base, line = place_of(length, alive)
        for i, own in enumerate((kb, vb)):
            load(i, j).wait()
            put_line(pairs[i][1], j, base, line, [own[k, j : j + 1].astype(jnp.float32) for k in range(KVH)])
            store(i, j).start()
        own_heads = q32[:, j, :]
        normed = attend([own_heads[k * PER : (k + 1) * PER] for k in range(KVH)], kbuf, vbuf, j, length, gb[...])
        att[:, j, :] = jnp.where(alive, normed, 0.0)
    for j in range(slots):
        for i in range(2):
            store(i, j).wait()
    for copy in large:
        copy.wait()


def moved_kernel(send_slot, send_to, lengths, gain, att, given_row, spread, out, mine):
    me = lax.axis_index(GROUP)
    mine[...] = att[...]

    @pl.when(send_to[me] != me)
    def _():
        slots = mine.shape[1]
        given = send_slot[me]
        packet = spread[send_to[me], 0:TILE].astype(jnp.float32)

        def by_head(first, last):
            return [packet[first:last, k * HD : (k + 1) * HD] for k in range(KVH)]

        token = (by_head(PER, PER + 1), by_head(PER + 1, PER + 2))
        rows = (given_row.at[0:1], given_row.at[1:2])
        normed = attend(by_head(0, PER), *rows, 0, lengths[given], gain[...], token)
        for j in range(slots):
            pl.when(given == j)(lambda j=j: mine.__setitem__((slice(None), j, slice(None)), normed))

    for h in range(HQ):
        head = mine[h].astype(jnp.bfloat16)
        for c in range(out.shape[0]):
            out[c, :, h * HD : (h + 1) * HD] = head


def select_kernel(receive_from, spread, _, outgoing, piece_sem):
    n = outgoing.shape[0]

    def piece(d):
        return pltpu.make_async_copy(spread.at[receive_from[d]], outgoing.at[d, pl.ds(0, 2 * TILE)], piece_sem.at[d])

    for d in range(n):
        pl.when(receive_from[d] != d)(lambda d=d: piece(d).start())
    for d in range(n):
        pl.when(receive_from[d] != d)(lambda d=d: piece(d).wait())


def ffn_kernel(near, far, pick, gate_weight, up_weight, down_weight, hidden, theirs, up_v, down_v, sems):
    width = theirs.shape[1]
    step = up_v.shape[0] // CHUNKS
    side = pl.ds(pl.multiple_of((1 - lax.axis_index("core")) * width, width), width)
    chunks = [pl.ds(c * step, step) for c in range(CHUNKS)]
    ups = [pltpu.make_async_copy(up_weight.at[at], up_v.at[at], sems.at[c]) for c, at in enumerate(chunks)]
    down = pltpu.make_async_copy(down_weight.at[:, side], down_v, sems.at[CHUNKS])
    for load in ups + [down]:
        load.start()
    x = jnp.concatenate([near[...], far[...]], axis=0)
    gate = jnp.dot(x, gate_weight[...], preferred_element_type=jnp.float32)
    up_part = 0.0
    for c in range(CHUNKS):
        at = slice(c * step, (c + 1) * step)
        x = jnp.concatenate([near[:, at], far[:, at]], axis=0)
        ups[c].wait()
        up_part += jnp.dot(x, up_v[at], preferred_element_type=jnp.float32)
    placed = (gate / (1.0 + jnp.exp(-gate)) * up_part).astype(jnp.bfloat16)
    placed = jnp.dot(pick[...], placed, preferred_element_type=jnp.float32).astype(jnp.bfloat16)
    hidden[...] = placed
    down.wait()
    theirs[...] = jnp.dot(placed, down_v[...], preferred_element_type=jnp.float32).astype(jnp.bfloat16)


def own_half_kernel(hidden, down_weight, mine, down_v, sem):
    width = mine.shape[1]
    side = pl.ds(pl.multiple_of(lax.axis_index("core") * width, width), width)
    down = pltpu.make_async_copy(down_weight.at[:, side], down_v, sem)
    down.start()
    down.wait()
    mine[...] = jnp.dot(hidden[...], down_v[...], preferred_element_type=jnp.float32)


def place_kernel(mine, theirs, outgoing, out, rows, sem):
    n, _, wide = rows.shape
    slots = mine.shape[0] // n
    for d in range(n):
        at = slice(d * slots, (d + 1) * slots)
        both = mine[at] + theirs[at].astype(jnp.float32)
        rows[d] = jnp.concatenate(
            [both[:, g * wide : (g + 1) * wide] for g in range(both.shape[1] // wide)], axis=0
        ).astype(jnp.bfloat16)
    copy = pltpu.make_async_copy(rows, out.at[:, pl.ds(2 * TILE, TILE)], sem)
    copy.start()
    copy.wait()


def finish_kernel(
    receive_from, land_slot, land_length, nk, nv, arrived, keys_in, values_in, decoded, keys, values, whole, sums, sems
):
    me = lax.axis_index(GROUP)
    n, wide = arrived.shape[0], arrived.shape[2]
    slots, slot = decoded.shape[0], land_slot[me]
    arriving = receive_from[me] != me
    length = land_length[me]
    block = length // TILE
    outs = ((keys, nk), (values, nv))
    stores = [pltpu.make_async_copy(whole.at[i], outs[i][0].at[slot], sems.at[i]) for i in range(2)]

    @pl.when(arriving)
    def _():
        here = lax.broadcasted_iota(jnp.int32, (TILE, HD), 0) == length - block * TILE
        for i in range(2):
            own = outs[i][1]
            mine = lax.broadcasted_iota(jnp.int32, (KVH, slots, HD), 1) == slot
            token = jnp.sum(jnp.where(mine, own[...].astype(jnp.float32), 0.0), axis=1)
            for d in range(n):
                whole[i, d] = arrived[d, i * TILE : (i + 1) * TILE]
            for k in range(KVH):
                columns = slice(k * HD, (k + 1) * HD)
                old = arrived[block, i * TILE : (i + 1) * TILE, columns].astype(jnp.float32)
                whole[i, block, :, columns] = jnp.where(here, token[k : k + 1], old).astype(jnp.bfloat16)
            stores[i].start()

    for side in range(2):
        total = arrived[side, 2 * TILE : 3 * TILE].astype(jnp.float32)
        for c in range(1, n // 2):
            total += arrived[2 * c + side, 2 * TILE : 3 * TILE].astype(jnp.float32)
        for g in range(TILE // slots):
            at = (side * (TILE // slots) + g) * wide
            sums[:, at : at + wide] = total[g * slots : (g + 1) * slots].astype(jnp.bfloat16)
    finished = pltpu.make_async_copy(sums, decoded, sems.at[2])
    finished.start()

    @pl.when(arriving)
    def _():
        for store in stores:
            store.wait()

    finished.wait()


def per_device(
    cache_keys, cache_values, lengths, unfinished, send_slot, send_to, receive_from, land_slot, land_length,
    queries, new_keys, new_values, norm_gain, gate_weight, up_weight, down_weight
):
    chips, n = lax.axis_size("chip"), lax.axis_size(GROUP)
    slots, capacity, kv_width = cache_keys.shape
    width = queries.shape[1]
    if capacity != TILE * n or slots * width != 2 * TILE * kv_width:
        return per_device_small_pieces(
            cache_keys, cache_values, lengths, unfinished, send_slot, send_to, receive_from, land_slot, land_length,
            queries, new_keys, new_values, norm_gain, gate_weight, up_weight, down_weight
        )
    bf16, f32, i32 = jnp.bfloat16, jnp.float32, jnp.int32
    dma = pltpu.SemaphoreType.DMA
    pieces = (slots, n, TILE, kv_width)
    room = pltpu.CompilerParams(vmem_limit_bytes=16 * 2**20)
    hbm = spec(pltpu.HBM)

    def shape(dims, kind=bf16):
        return jax.ShapeDtypeStruct(dims, kind)

    def by_head(x):
        return x.reshape(slots, -1, HD).transpose(1, 0, 2)

    q, nk, nv = by_head(queries), by_head(new_keys), by_head(new_values)
    gain = norm_gain.reshape(HQ, HD)
    tokens = [VMEM(q.shape, bf16), VMEM(nk.shape, bf16), VMEM(nv.shape, bf16)]
    leaving = pl.pallas_call(
        pack_kernel,
        out_shape=shape((n, 2 * TILE, kv_width)),
        in_specs=[hbm] * 9,
        out_specs=hbm,
        scratch_shapes=[SMEM((n,), i32)] * 4 + tokens + [
            VMEM((2,) + pieces, bf16), VMEM((TILE, kv_width), f32), VMEM((TILE, kv_width), bf16), dma((11,))
        ],
        compiler_params=pltpu.CompilerParams(vmem_limit_bytes=60 * 2**20),
        cost_estimate=cost(0, 2**20),
        name="pack",
    )(
        send_slot, send_to, receive_from, land_slot, q, nk, nv, cache_keys.reshape(pieces), cache_values.reshape(pieces)
    )
    spread = exchange(leaving, GROUP)
    att, keys_own, values_own, given_row, pick = pl.pallas_call(
        local_kernel,
        out_shape=(
            shape((HQ, slots, HD), f32),
            shape(cache_keys.shape),
            shape(cache_keys.shape),
            shape((2, capacity, kv_width)),
            shape((n * slots, n * slots)),
        ),
        in_specs=[hbm] * 12,
        out_specs=(spec(VMEM), hbm, hbm, spec(VMEM), spec(VMEM)),
        scratch_shapes=[SMEM((n,), i32)] * 4 + [SMEM((slots,), i32)] * 2 + tokens + [
            VMEM((HQ, HD), f32),
            VMEM((HQ, slots, HD), f32),
            VMEM(cache_keys.shape, bf16),
            VMEM(cache_keys.shape, bf16),
            dma((2, slots)),
            dma((10,)),
            dma((2,)),
        ],
        compiler_params=room,
        cost_estimate=cost(2**24, 2**24),
        name="local",
    )(
        send_slot, send_to, receive_from, land_slot, lengths, unfinished, q, nk, nv, gain, cache_keys, cache_values
    )
    rows = pl.pallas_call(
        moved_kernel,
        out_shape=shape((chips, slots, width)),
        in_specs=[spec(SMEM)] * 3 + [spec(VMEM)] * 4,
        out_specs=spec(VMEM),
        scratch_shapes=[VMEM((HQ, slots, HD), f32)],
        compiler_params=room,
        cost_estimate=cost(2**22, 2**20),
        name="moved",
    )(send_slot, send_to, lengths, gain, att, given_row, spread)
    near = exchange(rows, "chip")
    near = near.reshape(chips * slots, width)
    far = lax.ppermute(near, "core", [(0, 1), (1, 0)])
    outgoing = pl.pallas_call(
        select_kernel,
        out_shape=shape((n, 3 * TILE, kv_width)),
        in_specs=[spec(SMEM)] + [spec(pl.ANY)] * 2,
        out_specs=spec(pl.ANY),
        scratch_shapes=[dma((n,))],
        compiler_params=room,
        cost_estimate=cost(0, 2**20),
        name="select",
    )(receive_from, spread, near)
    far, outgoing = lax.optimization_barrier((far, outgoing))
    units = gate_weight.shape[1]
    hidden, theirs = pl.pallas_call(
        ffn_kernel,
        out_shape=(shape((n * slots, units)), shape((n * slots, width // 2))),
        in_specs=[spec(VMEM)] * 4 + [hbm] * 2,
        out_specs=(spec(VMEM), spec(VMEM)),
        scratch_shapes=[VMEM(up_weight.shape, bf16), VMEM((units, width // 2), bf16), dma((CHUNKS + 1,))],
        compiler_params=pltpu.CompilerParams(vmem_limit_bytes=50 * 2**20),
        cost_estimate=cost(5 * n * slots * width * units, 3 * 2**21),
        name="ffn",
    )(near, far, pick, gate_weight, up_weight, down_weight)
    mine = pl.pallas_call(
        own_half_kernel,
        out_shape=shape((n * slots, width // 2), f32),
        in_specs=[spec(VMEM), hbm],
        out_specs=spec(VMEM),
        scratch_shapes=[VMEM((units, width // 2), bf16), dma],
        compiler_params=pltpu.CompilerParams(vmem_limit_bytes=52 * 2**20),
        cost_estimate=cost(n * slots * width * units, 2**20),
        name="own_half",
    )(hidden, down_weight)
    theirs = lax.ppermute(theirs, "core", [(0, 1), (1, 0)])
    outgoing = pl.pallas_call(
        place_kernel,
        out_shape=shape((n, 3 * TILE, kv_width)),
        in_specs=[spec(VMEM)] * 2 + [spec(pl.ANY)],
        out_specs=spec(pl.ANY),
        scratch_shapes=[VMEM((n, TILE, kv_width), bf16), dma],
        input_output_aliases={2: 0},
        compiler_params=room,
        cost_estimate=cost(0, 2**20),
        name="place",
    )(mine, theirs, outgoing)
    arrived = exchange(outgoing, GROUP)
    decoded, keys_after, values_after = pl.pallas_call(
        finish_kernel,
        out_shape=(shape((slots, width)), shape(pieces), shape(pieces)),
        in_specs=[spec(SMEM)] * 3 + [spec(VMEM)] * 3 + [spec(pl.ANY)] * 2,
        out_specs=(hbm, spec(pl.ANY), spec(pl.ANY)),
        scratch_shapes=[VMEM((2, n, TILE, kv_width), bf16), VMEM((slots, width), bf16), dma((3,))],
        input_output_aliases={6: 1, 7: 2},
        compiler_params=room,
        cost_estimate=cost(0, 2**20),
        name="finish",
    )(
        receive_from, land_slot, land_length, nk, nv, arrived, keys_own.reshape(pieces), values_own.reshape(pieces)
    )
    return (decoded, keys_after.reshape(cache_keys.shape), values_after.reshape(cache_keys.shape))


def per_device_small_pieces(
    cache_keys,
    cache_values,
    lengths,
    unfinished,
    send_slot,
    send_to,
    receive_from,
    land_slot,
    land_length,
    queries,
    new_keys,
    new_values,
    norm_gain,
    gate_weight,
    up_weight,
    down_weight,
):
    group = GROUP
    me = lax.axis_index(group)
    chips, n = lax.axis_size("chip"), lax.axis_size(group)
    my_chip, my_core = lax.axis_index("chip"), lax.axis_index("core")
    slots, capacity, kv_width = cache_keys.shape
    width = queries.shape[1]
    slot_ids = jnp.arange(slots)
    target, source = send_to[me], receive_from[me]
    given_slot, taken_slot = send_slot[me], land_slot[me]
    giving, arriving = target != me, source != me
    landing = (slot_ids == taken_slot) & arriving
    vacated = (slot_ids == given_slot) & giving

    packet = jnp.concatenate(
        [
            lax.dynamic_index_in_dim(queries, taken_slot, 0, keepdims=False),
            lax.dynamic_index_in_dim(new_keys, taken_slot, 0, keepdims=False),
            lax.dynamic_index_in_dim(new_values, taken_slot, 0, keepdims=False),
        ]
    ).reshape(-1, 128)
    packets = exchange(jnp.broadcast_to(packet[None], (n,) + packet.shape), group)
    got = lax.dynamic_index_in_dim(packets, target, 0, keepdims=False).reshape(-1)

    rows = capacity // n
    leaving = jnp.concatenate(
        [
            lax.dynamic_index_in_dim(cache_keys, given_slot, 0, keepdims=False).reshape(n, rows, kv_width),
            lax.dynamic_index_in_dim(cache_values, given_slot, 0, keepdims=False).reshape(n, rows, kv_width),
        ],
        axis=1,
    )
    spread = exchange(leaving, group)

    row_queries = jnp.where(vacated[:, None], got[None, :width], queries)
    row_keys = jnp.where(vacated[:, None], got[None, width : width + kv_width], new_keys)
    row_values = jnp.where(vacated[:, None], got[None, width + kv_width :], new_values)
    row_alive = jnp.where(vacated, 1, jnp.where(landing, 0, unfinished)) > 0
    positions = jnp.arange(capacity)
    append = (positions[None, :] == lengths[:, None]) & row_alive[:, None]
    keys_here = jnp.where(append[:, :, None], row_keys[:, None, :], cache_keys)
    values_here = jnp.where(append[:, :, None], row_values[:, None, :], cache_values)
    query_heads = row_queries.reshape(slots, KVH, HQ // KVH, HD)
    key_heads = keys_here.reshape(slots, capacity, KVH, HD)
    value_heads = values_here.reshape(slots, capacity, KVH, HD)
    scores = jnp.einsum(
        "skgd,sckd->skgc", query_heads, key_heads, preferred_element_type=jnp.float32
    ) * (1.0 / math.sqrt(HD))
    visible = (positions[None, :] <= lengths[:, None])[:, None, None, :]
    scores = jnp.where(visible, scores, jnp.float32(-1e30))
    top = jnp.max(scores, axis=-1, keepdims=True)
    expo = jnp.exp(scores - top)
    probs = (expo / jnp.sum(expo, axis=-1, keepdims=True)).astype(jnp.bfloat16)
    attended = jnp.einsum(
        "skgc,sckd->skgd", probs, value_heads, preferred_element_type=jnp.float32
    ).reshape(slots, HQ * HD)
    mean_square = jnp.mean(attended * attended, axis=-1, keepdims=True)
    normed = attended * lax.rsqrt(mean_square + 1e-06) * norm_gain[None, :]
    normed = jnp.where(row_alive[:, None], normed, 0.0).astype(jnp.bfloat16)

    by_chip = exchange(jnp.broadcast_to(normed[None], (chips,) + normed.shape), "chip")
    other = lax.ppermute(by_chip, "core", [(0, 1), (1, 0)])

    chosen = jnp.take(spread, jnp.clip(receive_from, 0, n - 1), axis=0)
    arrived = exchange(chosen, group)
    arrived_keys = arrived[:, :rows].reshape(capacity, kv_width)
    arrived_values = arrived[:, rows:].reshape(capacity, kv_width)
    length_now = jnp.where(landing, land_length[me], lengths)
    alive = jnp.where(vacated, 0, jnp.where(landing, 1, unfinished)) > 0
    append_now = (positions[None, :] == length_now[:, None]) & alive[:, None]
    keys_after = jnp.where(landing[:, None, None], arrived_keys[None], cache_keys)
    values_after = jnp.where(landing[:, None, None], arrived_values[None], cache_values)
    keys_after = jnp.where(append_now[:, :, None], new_keys[:, None, :], keys_after)
    values_after = jnp.where(append_now[:, :, None], new_values[:, None, :], values_after)

    gathered = jnp.concatenate([by_chip, other], axis=0).reshape(n * slots, width)
    gate = jnp.dot(gathered, gate_weight, preferred_element_type=jnp.float32)
    up_part = jnp.dot(gathered, up_weight, preferred_element_type=jnp.float32)
    hidden = (jax.nn.silu(gate) * up_part).astype(jnp.bfloat16)
    everyone = jnp.arange(n)
    arrives = receive_from != everyone
    gives = send_to != everyone
    row_of = everyone[:, None] * slots + slot_ids[None, :]
    from_row = jnp.where(
        arrives[:, None] & (slot_ids[None, :] == land_slot[:, None]),
        (receive_from * slots + jnp.take(send_slot, jnp.clip(receive_from, 0, n - 1)))[:, None],
        row_of,
    )
    from_row = jnp.where(gives[:, None] & (slot_ids[None, :] == send_slot[:, None]), -1, from_row)
    order = jnp.concatenate([jnp.arange(chips) * 2 + 1 - my_core, jnp.arange(chips) * 2 + my_core])
    held = jnp.concatenate([jnp.arange(chips) * 2 + my_core, jnp.arange(chips) * 2 + 1 - my_core])
    wanted = jnp.take(from_row, order, axis=0).reshape(-1)
    held_row = (held[:, None] * slots + slot_ids[None, :]).reshape(-1)
    pick = (wanted[:, None] == held_row[None, :]).astype(jnp.bfloat16)
    placed_hidden = jnp.dot(pick, hidden, preferred_element_type=jnp.float32).astype(jnp.bfloat16)
    partial = jnp.dot(placed_hidden, down_weight, preferred_element_type=jnp.float32)
    half = chips * slots
    from_other = lax.ppermute(partial[:half].astype(jnp.bfloat16), "core", [(0, 1), (1, 0)])
    chip_sum = (partial[half:] + from_other.astype(jnp.float32)).astype(jnp.bfloat16)
    pieces = exchange(chip_sum.reshape(chips, slots, width), "chip")
    decoded = jnp.sum(pieces.astype(jnp.float32), axis=0).astype(jnp.bfloat16)
    return (decoded, keys_after, values_after)


def solution(mesh):
    parts, n = mesh.shape["parts"], mesh.shape["dp"]
    split = jax.sharding.Mesh(mesh.devices.reshape(parts, n // 2, 2), ("parts", "chip", "core"))
    every, own = ("parts", "chip", "core"), ("chip", "core")
    placed = (
        P(every, None, None),
        P(every, None, None),
        P(every),
        P(every),
        P("parts"),
        P("parts"),
        P("parts"),
        P("parts"),
        P("parts"),
        P(every, None),
        P(every, None),
        P(every, None),
        P(),
        P(None, own),
        P(None, own),
        P(own, None),
    )
    return jax.shard_map(
        per_device,
        mesh=split,
        in_specs=placed,
        out_specs=(P(every, None), P(every, None, None), P(every, None, None)),
        check_vma=False,
    )
```

```python
import math

import jax
import jax.numpy as jnp
from jax import lax
from jax.experimental import pallas as pl
from jax.experimental.pallas import tpu as pltpu
from jax.sharding import PartitionSpec as P

HQ = 32
KVH = 4
HD = 128
PER = HQ // KVH
TILE = 16
CHUNKS = 2
GROUP = ("chip", "core")
SMEM, VMEM = pltpu.SMEM, pltpu.VMEM


def exchange(blocks, axis):
    return lax.all_to_all(blocks, axis, 0, 0, tiled=True)


def spec(space):
    return pl.BlockSpec(memory_space=space)


def cost(flops, moved):
    return pl.CostEstimate(flops=flops, bytes_accessed=moved, transcendentals=0)


def pack_kernel(
    send_slot, send_to, receive_from, land_slot, q, nk, nv, ck, cv, leaving,
    slot_s, to_s, from_s, land_s, qb, kb, vb, whole, packet, tile, sems
):
    me = lax.axis_index(GROUP)
    slots = q.shape[1]
    fetches = [
        pltpu.make_async_copy(a, b, sems.at[2 + i])
        for i, (a, b) in enumerate(
            (
                (send_slot, slot_s), (send_to, to_s), (receive_from, from_s), (land_slot, land_s),
                (q, qb), (nk, kb), (nv, vb),
            )
        )
    ]
    for fetch in fetches:
        fetch.start()
    loads = [pltpu.make_async_copy(cache, whole.at[i], sems.at[i]) for i, cache in enumerate((ck, cv))]
    for load in loads:
        load.start()
    for fetch in fetches:
        fetch.wait()
    giving = to_s[me] != me
    stores = [
        pltpu.make_async_copy(whole.at[i, slot_s[me]], leaving.at[:, pl.ds(i * TILE, TILE)], sems.at[9 + i]) for i in range(2)
    ]

    for load, store in zip(loads, stores):
        load.wait()
        pl.when(giving)(store.start)

    @pl.when(giving)
    def _():
        for store in stores:
            store.wait()

    @pl.when(jnp.logical_not(giving))
    def _():
        taken = land_s[me]

        def line(x):
            mine = lax.broadcasted_iota(jnp.int32, (x.shape[0], slots, HD), 1) == taken
            return jnp.sum(jnp.where(mine, x[...].astype(jnp.float32), 0.0), axis=1)

        heads, key, value = line(qb), line(kb), line(vb)
        packet[...] = jnp.zeros_like(packet)
        for k in range(KVH):
            columns = slice(k * HD, (k + 1) * HD)
            packet[0:PER, columns] = heads[k * PER : (k + 1) * PER]
            packet[PER : PER + 1, columns] = key[k : k + 1]
            packet[PER + 1 : PER + 2, columns] = value[k : k + 1]
        tile[...] = packet[...].astype(jnp.bfloat16)
        send = pltpu.make_async_copy(tile, leaving.at[from_s[me], pl.ds(0, TILE)], sems.at[0])
        send.start()
        send.wait()


def put_line(buf, at, base, line, fresh):
    here = lax.broadcasted_iota(jnp.int32, (TILE, HD), 0) == line
    for k in range(KVH):
        columns = slice(k * HD, (k + 1) * HD)
        old = buf[at, pl.ds(base, TILE), columns].astype(jnp.float32)
        buf[at, pl.ds(base, TILE), columns] = jnp.where(here, fresh[k], old).astype(jnp.bfloat16)


def place_of(length, alive):
    block = length // TILE
    return pl.multiple_of(block * TILE, TILE), jnp.where(alive, length - block * TILE, -1)


def attend(heads, kbuf, vbuf, at, length, gain, token=None):
    scores = jnp.concatenate(
        [
            lax.dot_general(
                heads[k].astype(jnp.bfloat16),
                kbuf[at, :, k * HD : (k + 1) * HD],
                (((1,), (1,)), ((), ())),
                preferred_element_type=jnp.float32,
            )
            for k in range(KVH)
        ],
        axis=0,
    )
    position = lax.broadcasted_iota(jnp.int32, scores.shape, 1)
    if token is not None:
        fresh = [jnp.sum(heads[k] * token[0][k], axis=1, keepdims=True) for k in range(KVH)]
        scores = jnp.where(position == length, jnp.concatenate(fresh, axis=0), scores)
    scores = jnp.where(position <= length, scores * (1.0 / math.sqrt(HD)), jnp.float32(-1e30))
    expo = jnp.exp(scores - jnp.max(scores, axis=1, keepdims=True))
    probs = expo / jnp.sum(expo, axis=1, keepdims=True)
    if token is not None:
        last = jnp.sum(jnp.where(position == length, probs, 0.0), axis=1, keepdims=True)
        last = last.astype(jnp.bfloat16).astype(jnp.float32)
        probs = jnp.where(position == length, 0.0, probs)
    parts = [
        jnp.dot(
            probs[k * PER : (k + 1) * PER].astype(jnp.bfloat16),
            vbuf[at, :, k * HD : (k + 1) * HD],
            preferred_element_type=jnp.float32,
        )
        for k in range(KVH)
    ]
    if token is not None:
        parts = [parts[k] + last[k * PER : (k + 1) * PER] * token[1][k] for k in range(KVH)]
    attended = jnp.concatenate(parts, axis=0)
    mean = jnp.sum(attended * attended, keepdims=True) * (1.0 / (HQ * HD))
    return attended * lax.rsqrt(mean + 1e-06) * gain


def local_kernel(
    send_slot, send_to, receive_from, land_slot, lengths, unfinished, q, nk, nv, gain, ck, cv,
    att, keys, values, given_row, pick,
    slot_s, to_s, from_s, land_s, length_s, left_s, qb, kb, vb, gb, q32, kbuf, vbuf, sems, small, big
):
    me = lax.axis_index(GROUP)
    core = lax.axis_index("core")
    slots, n, rows = ck.shape[0], slot_s.shape[0], pick.shape[0]
    half = rows // 2
    pairs = ((ck, kbuf, keys), (cv, vbuf, values))
    fetches = [
        pltpu.make_async_copy(a, b, small.at[i])
        for i, (a, b) in enumerate(
            (
                (send_slot, slot_s), (send_to, to_s), (receive_from, from_s), (land_slot, land_s),
                (lengths, length_s), (unfinished, left_s), (q, qb), (nk, kb), (nv, vb), (gain, gb),
            )
        )
    ]
    for fetch in fetches:
        fetch.start()

    def load(i, j):
        return pltpu.make_async_copy(pairs[i][0].at[j], pairs[i][1].at[j], sems.at[i, j])

    def store(i, j):
        return pltpu.make_async_copy(pairs[i][1].at[j], pairs[i][2].at[j], sems.at[i, j])

    for j in range(slots):
        for i in range(2):
            load(i, j).start()
    for fetch in fetches:
        fetch.wait()
    large = [pltpu.make_async_copy(pairs[i][0].at[slot_s[me]], given_row.at[i], big.at[i]) for i in range(2)]
    for copy in large:
        copy.start()
    row = lax.broadcasted_iota(jnp.int32, (rows, HD), 0)
    device = row // slots
    wanted = jnp.where((device & 1) == core, 0, half) + (device >> 1) * slots + (row & (slots - 1))
    for d in range(n):
        source = from_s[d]
        held = jnp.where(lax.rem(source, 2) == core, 0, half) + (source // 2) * slots + slot_s[source]
        landing = jnp.where(source != d, d * slots + land_s[d], -1)
        vacated = jnp.where(to_s[d] != d, d * slots + slot_s[d], -1)
        wanted = jnp.where(row == landing, held, wanted)
        wanted = jnp.where(row == vacated, -1, wanted)
    column = lax.broadcasted_iota(jnp.int32, (rows, rows), 1)
    pick[...] = (column == wanted[:, :1]).astype(jnp.float32).astype(jnp.bfloat16)
    q32[...] = qb[...].astype(jnp.float32)
    for j in range(slots):
        vacated = (to_s[me] != me) & (slot_s[me] == j)
        alive = jnp.where(vacated, 0, left_s[j]) > 0
        length = length_s[j]
        base, line = place_of(length, alive)
        for i, own in enumerate((kb, vb)):
            load(i, j).wait()
            put_line(pairs[i][1], j, base, line, [own[k, j : j + 1].astype(jnp.float32) for k in range(KVH)])
            store(i, j).start()
        own_heads = q32[:, j, :]
        normed = attend([own_heads[k * PER : (k + 1) * PER] for k in range(KVH)], kbuf, vbuf, j, length, gb[...])
        att[:, j, :] = jnp.where(alive, normed, 0.0)
    for j in range(slots):
        for i in range(2):
            store(i, j).wait()
    for copy in large:
        copy.wait()


def moved_kernel(send_slot, send_to, lengths, gain, att, given_row, spread, out, mine):
    me = lax.axis_index(GROUP)
    mine[...] = att[...]

    @pl.when(send_to[me] != me)
    def _():
        slots = mine.shape[1]
        given = send_slot[me]
        packet = spread[send_to[me], 0:TILE].astype(jnp.float32)

        def by_head(first, last):
            return [packet[first:last, k * HD : (k + 1) * HD] for k in range(KVH)]

        token = (by_head(PER, PER + 1), by_head(PER + 1, PER + 2))
        rows = (given_row.at[0:1], given_row.at[1:2])
        normed = attend(by_head(0, PER), *rows, 0, lengths[given], gain[...], token)
        for j in range(slots):
            pl.when(given == j)(lambda j=j: mine.__setitem__((slice(None), j, slice(None)), normed))

    for h in range(HQ):
        head = mine[h].astype(jnp.bfloat16)
        for c in range(out.shape[0]):
            out[c, :, h * HD : (h + 1) * HD] = head


def select_kernel(receive_from, spread, up_weight, _, outgoing, up_v, piece_sem, sem):
    n = outgoing.shape[0]
    up = pltpu.make_async_copy(up_weight.at[pl.ds(0, up_v.shape[0])], up_v, sem)

    def piece(d):
        return pltpu.make_async_copy(spread.at[receive_from[d]], outgoing.at[d, pl.ds(0, 2 * TILE)], piece_sem.at[d])

    up.start()
    for d in range(n):
        pl.when(receive_from[d] != d)(lambda d=d: piece(d).start())
    for d in range(n):
        pl.when(receive_from[d] != d)(lambda d=d: piece(d).wait())
    up.wait()


def ffn_kernel(near, far, pick, gate_weight, first_up, up_weight, down_weight, hidden, theirs, up_v, down_v, sems):
    width = theirs.shape[1]
    first = first_up.shape[0]
    step = up_v.shape[0] // CHUNKS
    side = pl.ds(pl.multiple_of((1 - lax.axis_index("core")) * width, width), width)
    chunks = [pl.ds(c * step, step) for c in range(CHUNKS)]
    ups = [
        pltpu.make_async_copy(up_weight.at[pl.ds(first + c * step, step)], up_v.at[at], sems.at[c])
        for c, at in enumerate(chunks)
    ]
    down = pltpu.make_async_copy(down_weight.at[:, side], down_v, sems.at[CHUNKS])
    for load in ups + [down]:
        load.start()
    x = jnp.concatenate([near[...], far[...]], axis=0)
    gate = jnp.dot(x, gate_weight[...], preferred_element_type=jnp.float32)
    up_part = jnp.dot(x[:, :first], first_up[...], preferred_element_type=jnp.float32)
    for c in range(CHUNKS):
        at = slice(first + c * step, first + (c + 1) * step)
        ups[c].wait()
        up_part += jnp.dot(x[:, at], up_v[chunks[c]], preferred_element_type=jnp.float32)
    placed = (gate / (1.0 + jnp.exp(-gate)) * up_part).astype(jnp.bfloat16)
    placed = jnp.dot(pick[...], placed, preferred_element_type=jnp.float32).astype(jnp.bfloat16)
    hidden[...] = placed
    down.wait()
    theirs[...] = jnp.dot(placed, down_v[...], preferred_element_type=jnp.float32).astype(jnp.bfloat16)


def own_half_kernel(hidden, down_weight, mine, down_v, sem):
    width = mine.shape[1]
    side = pl.ds(pl.multiple_of(lax.axis_index("core") * width, width), width)
    down = pltpu.make_async_copy(down_weight.at[:, side], down_v, sem)
    down.start()
    down.wait()
    mine[...] = jnp.dot(hidden[...], down_v[...], preferred_element_type=jnp.float32)


def place_kernel(mine, theirs, outgoing, out, rows, sem):
    n, _, wide = rows.shape
    slots = mine.shape[0] // n
    for d in range(n):
        at = slice(d * slots, (d + 1) * slots)
        both = mine[at] + theirs[at].astype(jnp.float32)
        rows[d] = jnp.concatenate(
            [both[:, g * wide : (g + 1) * wide] for g in range(both.shape[1] // wide)], axis=0
        ).astype(jnp.bfloat16)
    copy = pltpu.make_async_copy(rows, out.at[:, pl.ds(2 * TILE, TILE)], sem)
    copy.start()
    copy.wait()


def finish_kernel(
    receive_from, land_slot, land_length, nk, nv, arrived, keys_in, values_in, decoded, keys, values, whole, sums, sems
):
    me = lax.axis_index(GROUP)
    n, wide = arrived.shape[0], arrived.shape[2]
    slots, slot = decoded.shape[0], land_slot[me]
    arriving = receive_from[me] != me
    length = land_length[me]
    block = length // TILE
    outs = ((keys, nk), (values, nv))
    stores = [pltpu.make_async_copy(whole.at[i], outs[i][0].at[slot], sems.at[i]) for i in range(2)]

    @pl.when(arriving)
    def _():
        here = lax.broadcasted_iota(jnp.int32, (TILE, HD), 0) == length - block * TILE
        for i in range(2):
            own = outs[i][1]
            mine = lax.broadcasted_iota(jnp.int32, (KVH, slots, HD), 1) == slot
            token = jnp.sum(jnp.where(mine, own[...].astype(jnp.float32), 0.0), axis=1)
            for d in range(n):
                whole[i, d] = arrived[d, i * TILE : (i + 1) * TILE]
            for k in range(KVH):
                columns = slice(k * HD, (k + 1) * HD)
                old = arrived[block, i * TILE : (i + 1) * TILE, columns].astype(jnp.float32)
                whole[i, block, :, columns] = jnp.where(here, token[k : k + 1], old).astype(jnp.bfloat16)
            stores[i].start()

    for side in range(2):
        total = arrived[side, 2 * TILE : 3 * TILE].astype(jnp.float32)
        for c in range(1, n // 2):
            total += arrived[2 * c + side, 2 * TILE : 3 * TILE].astype(jnp.float32)
        for g in range(TILE // slots):
            at = (side * (TILE // slots) + g) * wide
            sums[:, at : at + wide] = total[g * slots : (g + 1) * slots].astype(jnp.bfloat16)
    finished = pltpu.make_async_copy(sums, decoded, sems.at[2])
    finished.start()

    @pl.when(arriving)
    def _():
        for store in stores:
            store.wait()

    finished.wait()


def per_device(
    cache_keys, cache_values, lengths, unfinished, send_slot, send_to, receive_from, land_slot, land_length,
    queries, new_keys, new_values, norm_gain, gate_weight, up_weight, down_weight
):
    chips, n = lax.axis_size("chip"), lax.axis_size(GROUP)
    slots, capacity, kv_width = cache_keys.shape
    width = queries.shape[1]
    if capacity != TILE * n or slots * width != 2 * TILE * kv_width:
        return per_device_small_pieces(
            cache_keys, cache_values, lengths, unfinished, send_slot, send_to, receive_from, land_slot, land_length,
            queries, new_keys, new_values, norm_gain, gate_weight, up_weight, down_weight
        )
    bf16, f32, i32 = jnp.bfloat16, jnp.float32, jnp.int32
    dma = pltpu.SemaphoreType.DMA
    pieces = (slots, n, TILE, kv_width)
    room = pltpu.CompilerParams(vmem_limit_bytes=16 * 2**20)
    hbm = spec(pltpu.HBM)

    def shape(dims, kind=bf16):
        return jax.ShapeDtypeStruct(dims, kind)

    def by_head(x):
        return x.reshape(slots, -1, HD).transpose(1, 0, 2)

    q, nk, nv = by_head(queries), by_head(new_keys), by_head(new_values)
    gain = norm_gain.reshape(HQ, HD)
    tokens = [VMEM(q.shape, bf16), VMEM(nk.shape, bf16), VMEM(nv.shape, bf16)]
    leaving = pl.pallas_call(
        pack_kernel,
        out_shape=shape((n, 2 * TILE, kv_width)),
        in_specs=[hbm] * 9,
        out_specs=hbm,
        scratch_shapes=[SMEM((n,), i32)] * 4 + tokens + [
            VMEM((2,) + pieces, bf16), VMEM((TILE, kv_width), f32), VMEM((TILE, kv_width), bf16), dma((11,))
        ],
        compiler_params=pltpu.CompilerParams(vmem_limit_bytes=60 * 2**20),
        cost_estimate=cost(0, 2**20),
        name="pack",
    )(
        send_slot, send_to, receive_from, land_slot, q, nk, nv, cache_keys.reshape(pieces), cache_values.reshape(pieces)
    )
    spread = exchange(leaving, GROUP)
    att, keys_own, values_own, given_row, pick = pl.pallas_call(
        local_kernel,
        out_shape=(
            shape((HQ, slots, HD), f32),
            shape(cache_keys.shape),
            shape(cache_keys.shape),
            shape((2, capacity, kv_width)),
            shape((n * slots, n * slots)),
        ),
        in_specs=[hbm] * 12,
        out_specs=(spec(VMEM), hbm, hbm, spec(VMEM), spec(VMEM)),
        scratch_shapes=[SMEM((n,), i32)] * 4 + [SMEM((slots,), i32)] * 2 + tokens + [
            VMEM((HQ, HD), f32),
            VMEM((HQ, slots, HD), f32),
            VMEM(cache_keys.shape, bf16),
            VMEM(cache_keys.shape, bf16),
            dma((2, slots)),
            dma((10,)),
            dma((2,)),
        ],
        compiler_params=pltpu.CompilerParams(vmem_limit_bytes=52 * 2**20),
        cost_estimate=cost(2**24, 2**24),
        name="local",
    )(
        send_slot, send_to, receive_from, land_slot, lengths, unfinished, q, nk, nv, gain, cache_keys, cache_values
    )
    rows = pl.pallas_call(
        moved_kernel,
        out_shape=shape((chips, slots, width)),
        in_specs=[spec(SMEM)] * 3 + [spec(VMEM)] * 4,
        out_specs=spec(VMEM),
        scratch_shapes=[VMEM((HQ, slots, HD), f32)],
        compiler_params=room,
        cost_estimate=cost(2**22, 2**20),
        name="moved",
    )(send_slot, send_to, lengths, gain, att, given_row, spread)
    near = exchange(rows, "chip")
    near = near.reshape(chips * slots, width)
    far = lax.ppermute(near, "core", [(0, 1), (1, 0)])
    units = gate_weight.shape[1]
    outgoing, up_v = pl.pallas_call(
        select_kernel,
        out_shape=(shape((n, 3 * TILE, kv_width)), shape((width // 2, units))),
        in_specs=[spec(SMEM), spec(pl.ANY), hbm, spec(pl.ANY)],
        out_specs=(spec(pl.ANY), spec(VMEM)),
        scratch_shapes=[dma((n,)), dma],
        compiler_params=room,
        cost_estimate=cost(0, 2**20),
        name="select",
    )(receive_from, spread, up_weight, near)
    far, outgoing = lax.optimization_barrier((far, outgoing))
    hidden, theirs = pl.pallas_call(
        ffn_kernel,
        out_shape=(shape((n * slots, units)), shape((n * slots, width // 2))),
        in_specs=[spec(VMEM)] * 5 + [hbm] * 2,
        out_specs=(spec(VMEM), spec(VMEM)),
        scratch_shapes=[VMEM((width // 2, units), bf16), VMEM((units, width // 2), bf16), dma((CHUNKS + 1,))],
        compiler_params=pltpu.CompilerParams(vmem_limit_bytes=50 * 2**20),
        cost_estimate=cost(5 * n * slots * width * units, 3 * 2**21),
        name="ffn",
    )(near, far, pick, gate_weight, up_v, up_weight, down_weight)
    mine = pl.pallas_call(
        own_half_kernel,
        out_shape=shape((n * slots, width // 2), f32),
        in_specs=[spec(VMEM), hbm],
        out_specs=spec(VMEM),
        scratch_shapes=[VMEM((units, width // 2), bf16), dma],
        compiler_params=pltpu.CompilerParams(vmem_limit_bytes=52 * 2**20),
        cost_estimate=cost(n * slots * width * units, 2**20),
        name="own_half",
    )(hidden, down_weight)
    theirs = lax.ppermute(theirs, "core", [(0, 1), (1, 0)])
    outgoing = pl.pallas_call(
        place_kernel,
        out_shape=shape((n, 3 * TILE, kv_width)),
        in_specs=[spec(VMEM)] * 2 + [spec(pl.ANY)],
        out_specs=spec(pl.ANY),
        scratch_shapes=[VMEM((n, TILE, kv_width), bf16), dma],
        input_output_aliases={2: 0},
        compiler_params=room,
        cost_estimate=cost(0, 2**20),
        name="place",
    )(mine, theirs, outgoing)
    arrived = exchange(outgoing, GROUP)
    decoded, keys_after, values_after = pl.pallas_call(
        finish_kernel,
        out_shape=(shape((slots, width)), shape(pieces), shape(pieces)),
        in_specs=[spec(SMEM)] * 3 + [spec(VMEM)] * 3 + [spec(pl.ANY)] * 2,
        out_specs=(hbm, spec(pl.ANY), spec(pl.ANY)),
        scratch_shapes=[VMEM((2, n, TILE, kv_width), bf16), VMEM((slots, width), bf16), dma((3,))],
        input_output_aliases={6: 1, 7: 2},
        compiler_params=room,
        cost_estimate=cost(0, 2**20),
        name="finish",
    )(
        receive_from, land_slot, land_length, nk, nv, arrived, keys_own.reshape(pieces), values_own.reshape(pieces)
    )
    return (decoded, keys_after.reshape(cache_keys.shape), values_after.reshape(cache_keys.shape))


def per_device_small_pieces(
    cache_keys,
    cache_values,
    lengths,
    unfinished,
    send_slot,
    send_to,
    receive_from,
    land_slot,
    land_length,
    queries,
    new_keys,
    new_values,
    norm_gain,
    gate_weight,
    up_weight,
    down_weight,
):
    group = GROUP
    me = lax.axis_index(group)
    chips, n = lax.axis_size("chip"), lax.axis_size(group)
    my_chip, my_core = lax.axis_index("chip"), lax.axis_index("core")
    slots, capacity, kv_width = cache_keys.shape
    width = queries.shape[1]
    slot_ids = jnp.arange(slots)
    target, source = send_to[me], receive_from[me]
    given_slot, taken_slot = send_slot[me], land_slot[me]
    giving, arriving = target != me, source != me
    landing = (slot_ids == taken_slot) & arriving
    vacated = (slot_ids == given_slot) & giving

    packet = jnp.concatenate(
        [
            lax.dynamic_index_in_dim(queries, taken_slot, 0, keepdims=False),
            lax.dynamic_index_in_dim(new_keys, taken_slot, 0, keepdims=False),
            lax.dynamic_index_in_dim(new_values, taken_slot, 0, keepdims=False),
        ]
    ).reshape(-1, 128)
    packets = exchange(jnp.broadcast_to(packet[None], (n,) + packet.shape), group)
    got = lax.dynamic_index_in_dim(packets, target, 0, keepdims=False).reshape(-1)

    rows = capacity // n
    leaving = jnp.concatenate(
        [
            lax.dynamic_index_in_dim(cache_keys, given_slot, 0, keepdims=False).reshape(n, rows, kv_width),
            lax.dynamic_index_in_dim(cache_values, given_slot, 0, keepdims=False).reshape(n, rows, kv_width),
        ],
        axis=1,
    )
    spread = exchange(leaving, group)

    row_queries = jnp.where(vacated[:, None], got[None, :width], queries)
    row_keys = jnp.where(vacated[:, None], got[None, width : width + kv_width], new_keys)
    row_values = jnp.where(vacated[:, None], got[None, width + kv_width :], new_values)
    row_alive = jnp.where(vacated, 1, jnp.where(landing, 0, unfinished)) > 0
    positions = jnp.arange(capacity)
    append = (positions[None, :] == lengths[:, None]) & row_alive[:, None]
    keys_here = jnp.where(append[:, :, None], row_keys[:, None, :], cache_keys)
    values_here = jnp.where(append[:, :, None], row_values[:, None, :], cache_values)
    query_heads = row_queries.reshape(slots, KVH, HQ // KVH, HD)
    key_heads = keys_here.reshape(slots, capacity, KVH, HD)
    value_heads = values_here.reshape(slots, capacity, KVH, HD)
    scores = jnp.einsum(
        "skgd,sckd->skgc", query_heads, key_heads, preferred_element_type=jnp.float32
    ) * (1.0 / math.sqrt(HD))
    visible = (positions[None, :] <= lengths[:, None])[:, None, None, :]
    scores = jnp.where(visible, scores, jnp.float32(-1e30))
    top = jnp.max(scores, axis=-1, keepdims=True)
    expo = jnp.exp(scores - top)
    probs = (expo / jnp.sum(expo, axis=-1, keepdims=True)).astype(jnp.bfloat16)
    attended = jnp.einsum(
        "skgc,sckd->skgd", probs, value_heads, preferred_element_type=jnp.float32
    ).reshape(slots, HQ * HD)
    mean_square = jnp.mean(attended * attended, axis=-1, keepdims=True)
    normed = attended * lax.rsqrt(mean_square + 1e-06) * norm_gain[None, :]
    normed = jnp.where(row_alive[:, None], normed, 0.0).astype(jnp.bfloat16)

    by_chip = exchange(jnp.broadcast_to(normed[None], (chips,) + normed.shape), "chip")
    other = lax.ppermute(by_chip, "core", [(0, 1), (1, 0)])

    chosen = jnp.take(spread, jnp.clip(receive_from, 0, n - 1), axis=0)
    arrived = exchange(chosen, group)
    arrived_keys = arrived[:, :rows].reshape(capacity, kv_width)
    arrived_values = arrived[:, rows:].reshape(capacity, kv_width)
    length_now = jnp.where(landing, land_length[me], lengths)
    alive = jnp.where(vacated, 0, jnp.where(landing, 1, unfinished)) > 0
    append_now = (positions[None, :] == length_now[:, None]) & alive[:, None]
    keys_after = jnp.where(landing[:, None, None], arrived_keys[None], cache_keys)
    values_after = jnp.where(landing[:, None, None], arrived_values[None], cache_values)
    keys_after = jnp.where(append_now[:, :, None], new_keys[:, None, :], keys_after)
    values_after = jnp.where(append_now[:, :, None], new_values[:, None, :], values_after)

    gathered = jnp.concatenate([by_chip, other], axis=0).reshape(n * slots, width)
    gate = jnp.dot(gathered, gate_weight, preferred_element_type=jnp.float32)
    up_part = jnp.dot(gathered, up_weight, preferred_element_type=jnp.float32)
    hidden = (jax.nn.silu(gate) * up_part).astype(jnp.bfloat16)
    everyone = jnp.arange(n)
    arrives = receive_from != everyone
    gives = send_to != everyone
    row_of = everyone[:, None] * slots + slot_ids[None, :]
    from_row = jnp.where(
        arrives[:, None] & (slot_ids[None, :] == land_slot[:, None]),
        (receive_from * slots + jnp.take(send_slot, jnp.clip(receive_from, 0, n - 1)))[:, None],
        row_of,
    )
    from_row = jnp.where(gives[:, None] & (slot_ids[None, :] == send_slot[:, None]), -1, from_row)
    order = jnp.concatenate([jnp.arange(chips) * 2 + 1 - my_core, jnp.arange(chips) * 2 + my_core])
    held = jnp.concatenate([jnp.arange(chips) * 2 + my_core, jnp.arange(chips) * 2 + 1 - my_core])
    wanted = jnp.take(from_row, order, axis=0).reshape(-1)
    held_row = (held[:, None] * slots + slot_ids[None, :]).reshape(-1)
    pick = (wanted[:, None] == held_row[None, :]).astype(jnp.bfloat16)
    placed_hidden = jnp.dot(pick, hidden, preferred_element_type=jnp.float32).astype(jnp.bfloat16)
    partial = jnp.dot(placed_hidden, down_weight, preferred_element_type=jnp.float32)
    half = chips * slots
    from_other = lax.ppermute(partial[:half].astype(jnp.bfloat16), "core", [(0, 1), (1, 0)])
    chip_sum = (partial[half:] + from_other.astype(jnp.float32)).astype(jnp.bfloat16)
    pieces = exchange(chip_sum.reshape(chips, slots, width), "chip")
    decoded = jnp.sum(pieces.astype(jnp.float32), axis=0).astype(jnp.bfloat16)
    return (decoded, keys_after, values_after)


def solution(mesh):
    parts, n = mesh.shape["parts"], mesh.shape["dp"]
    split = jax.sharding.Mesh(mesh.devices.reshape(parts, n // 2, 2), ("parts", "chip", "core"))
    every, own = ("parts", "chip", "core"), ("chip", "core")
    placed = (
        P(every, None, None),
        P(every, None, None),
        P(every),
        P(every),
        P("parts"),
        P("parts"),
        P("parts"),
        P("parts"),
        P("parts"),
        P(every, None),
        P(every, None),
        P(every, None),
        P(),
        P(None, own),
        P(None, own),
        P(own, None),
    )
    return jax.shard_map(
        per_device,
        mesh=split,
        in_specs=placed,
        out_specs=(P(every, None), P(every, None, None), P(every, None, None)),
        check_vma=False,
    )
```
